512 devices in a mesh: req: 8 (over x, core), head: 4 (over y), ctx: 16 (over z).
Axes of the slice: x: 4, y: 4, z: 16, core: 2. Of those that a mesh axis runs over, the one named last changes fastest.
Arguments:
- xz: bfloat16 [128, 2, 16384], P('req', None, ('head', 'ctx')), may hold values from -6 to 6
- conv_state: bfloat16 [128, 3, 16384], P('req', None, ('head', 'ctx')), may hold values from -6 to 6
- ssm_state: float32 [128, 16, 16384], P('req', None, ('head', 'ctx')), may hold values from -6 to 6
- conv_weight: float32 [4, 16384], P(None, ('head', 'ctx')), may hold values from -3 to 3
- conv_bias: float32 [16384], P(('head', 'ctx')), may hold values from -3 to 3
- x_proj: bfloat16 [16384, 544], P(('head', 'ctx')), may hold values from -0.046875 to 0.046875
- dt_norm_gain: float32 [512], replicated, may hold values from 0.1 to 1.9
- dt_proj: bfloat16 [512, 16384], P(None, ('head', 'ctx')), may hold values from -0.25 to 0.25
- dt_bias: float32 [16384], P(('head', 'ctx')), may hold values from -2 to 1
- a_log: float32 [16, 16384], P(None, ('head', 'ctx')), may hold values from -3 to 2.5
- d_skip: float32 [16384], P(('head', 'ctx')), may hold values from 0.5 to 1.5
- query: bfloat16 [128, 8192], P(('req', 'ctx'), 'head'), may hold values from -16 to 16
- new_kv: bfloat16 [128, 2048], P(('req', 'ctx'), 'head'), may hold values from -6 to 6
- kv_pool: bfloat16 [2560, 64, 2048], P(('req', 'ctx'), None, 'head'), may hold values from -4 to 4
- page_sel: int32 [128, 16], P(('req', 'ctx')), may hold values from 0 to 319, as said below
- lengths: int32 [128], P(('req', 'ctx')), may hold values from 1 to 64
Outputs:
- mamba_out: bfloat16 [128, 16384], P('req', ('head', 'ctx'))
- new_state: float32 [128, 16, 16384], P('req', None, ('head', 'ctx'))
- attention_out: bfloat16 [128, 8192], P(('req', 'ctx'), 'head')
The draws below stay inside these ranges and needn't reach their ends.
Inputs may be any that keep to these rules, and one draw needn't show every extreme that they name: `page_sel`: entry c * 20 + s names slot s of the pool of context shard c in the request's group (the 16 requests on one index of req). A request's pages are distinct, no page belongs to two requests, and the first entry is the request's newest page. Each request has exactly 3 of its pages on 4 context shards, one page on 4 others and none on the rest; every context shard holds exactly 16 selected pages of its group.
All inputs are finite; a program needn't handle non-finite values.
Results may differ from the reference program's by a relative error of at most 0.017.
Values may be sent and summed in bfloat16 or wider, within the bound.
A program may use at most 64 MiB of HBM per device.

```python
import math
import jax
import jax.numpy as jnp
from jax import lax

INNER = 16384
STATE = 16
DT_RANK = 512
KERNEL = 4
Q_HEADS = 64
KV_HEADS = 8
HEAD_DIM = 128
PAGE = 64
REQ_ROWS = 1
TOPK = 16
POOL = 20
NREQ = 128
NPAGES = 2560


def shuffle_base(sub_key, base_counts):
    return jax.random.permutation(sub_key, base_counts)


def shuffle_range(sub_key, count):
    return jax.random.permutation(sub_key, count)


def shuffle_slots(sub_key, count):
    shuffled = jax.random.permutation(sub_key, count)
    leading = shuffled[0]
    swapped = jnp.where(shuffled == count - 1, leading, shuffled)
    return swapped.at[0].set(count - 1)


def page_layout(key):
    key = jax.random.fold_in(key, 101)
    shard_count = TOPK
    group_size = REQ_ROWS * TOPK
    group_count = NREQ // group_size
    key_pattern, key_shift, key_slots, key_order = jax.random.split(key, 4)
    base_counts = jnp.tile(jnp.array([3, 1, 0, 0], dtype=jnp.int32), shard_count // 4)
    pattern = jax.vmap(shuffle_base, in_axes=(0, None))(jax.random.split(key_pattern, group_count), base_counts)
    shifts = jax.vmap(shuffle_range, in_axes=(0, None))(jax.random.split(key_shift, group_count * REQ_ROWS), shard_count)
    shifts = shifts.reshape(group_count, REQ_ROWS, shard_count).transpose(0, 2, 1).reshape(group_count, group_size)
    shard_ids = jnp.arange(shard_count, dtype=jnp.int32)
    rotated = (shard_ids[None, None, :] + shifts[:, :, None]) % shard_count
    counts = jnp.take_along_axis(jnp.broadcast_to(pattern[:, None, :], (group_count, group_size, shard_count)), rotated, axis=2)
    running = jnp.cumsum(counts, axis=2)
    shard_of = jnp.sum((running[:, :, None, :] <= shard_ids[None, None, :, None]).astype(jnp.int32), axis=3)
    shard_flat = shard_of.reshape(group_count, group_size * shard_count)
    one_hot = (shard_flat[:, :, None] == shard_ids[None, None, :]).astype(jnp.int32)
    earlier = jnp.cumsum(one_hot, axis=1) - one_hot
    order_rank = jnp.sum(earlier * one_hot, axis=2)
    slot_perms = jax.vmap(shuffle_slots, in_axes=(0, None))(jax.random.split(key_slots, group_count * shard_count), POOL)
    slot_perms = slot_perms.reshape(group_count, shard_count, POOL)
    group_index = jnp.arange(group_count, dtype=jnp.int32)[:, None]
    slot_of = slot_perms[group_index, shard_flat, order_rank]
    listed = (shard_flat * POOL + slot_of).reshape(NREQ, shard_count)
    order = jax.vmap(shuffle_range, in_axes=(0, None))(jax.random.split(key_order, NREQ), shard_count)
    return jnp.take_along_axis(listed, order, axis=1).astype(jnp.int32)


def shared_part(key):
    key = jax.random.fold_in(key, 102)
    return jax.random.truncated_normal(key, -4.0, 4.0, (NREQ, KV_HEADS, HEAD_DIM), jnp.float32)


def draw_page_sel(key, part):
    listed = page_layout(key)
    return listed


def draw_lengths(key, part):
    key = jax.random.fold_in(key, 2)
    key_vals, key_high, key_step = jax.random.split(key, 3)
    filled = jax.random.randint(key_vals, (NREQ,), 1, PAGE + 1)
    high_row = jax.random.randint(key_high, (), 0, NREQ)
    low_row = (high_row + 1 + jax.random.randint(key_step, (), 0, NREQ - 1)) % NREQ
    filled = filled.at[high_row].set(PAGE).at[low_row].set(1)
    return filled.astype(jnp.int32)


def draw_query(key, part):
    common = shared_part(key)
    key = jax.random.fold_in(key, 3)
    per_group = Q_HEADS // KV_HEADS
    shape = (NREQ, KV_HEADS, per_group, HEAD_DIM)
    noise = jax.random.truncated_normal(key, -4.0, 4.0, shape, jnp.float32)
    heads = 2.0 * (0.6 * common[:, :, None, :] + 0.8 * noise)
    return heads.reshape(NREQ, Q_HEADS * HEAD_DIM).astype(jnp.bfloat16)


def draw_new_kv(key, part):
    common = shared_part(key)
    key = jax.random.fold_in(key, 4)
    key_k, key_v = jax.random.split(key)
    shape = (NREQ, KV_HEADS, HEAD_DIM)
    noise = jax.random.truncated_normal(key_k, -4.0, 4.0, shape, jnp.float32)
    fresh_values = jax.random.truncated_normal(key_v, -4.0, 4.0, shape, jnp.float32)
    fresh_keys = 0.45 * common + 0.89 * noise
    stacked = jnp.stack([fresh_keys, fresh_values], axis=2)
    return stacked.reshape(NREQ, 2 * KV_HEADS * HEAD_DIM).astype(jnp.bfloat16)


def draw_kv_pool(key, part):
    key = jax.random.fold_in(key, 5)
    shape = (NPAGES, PAGE, KV_HEADS, 2, HEAD_DIM)
    pooled = jax.random.truncated_normal(key, -4.0, 4.0, shape, jnp.float32)
    return pooled.reshape(NPAGES, PAGE, 2 * KV_HEADS * HEAD_DIM).astype(jnp.bfloat16)


def level_of(own_key, shape, cuts, low, largest):
    def one(axis_at, blocks):
        steps = jax.random.uniform(jax.random.fold_in(jax.random.fold_in(own_key, 6), axis_at), (blocks,), jnp.float32, low / len(cuts), largest / len(cuts))
        return jnp.repeat(jnp.exp(steps), shape[axis_at] // blocks).reshape((-1,) + (1,) * (len(shape) - axis_at - 1))

    gain = one(*cuts[0])
    for cut in cuts[1:]:
        gain = gain * one(*cut)
    return gain


def scatter_about(key, extent, deviation, limit, shards=(), kind=jnp.bfloat16):
    values = deviation * jax.random.normal(key, extent, jnp.float32)
    if shards:
        values = values * level_of(key, extent, shards, -0.22, 0.18)
    return jnp.clip(values, -limit, limit).astype(kind)


def setup_inputs(seed: int = 0) -> dict:
    keys = jax.random.split(jax.random.key(seed), 17)
    return {
        "xz": scatter_about(keys[0], (NREQ, 2, INNER), 1.0, 6.0, ((0, 8), (2, 64))),
        "conv_state": scatter_about(keys[1], (NREQ, KERNEL - 1, INNER), 1.0, 6.0, ((0, 8), (2, 64))),
        "ssm_state": scatter_about(keys[2], (NREQ, STATE, INNER), 1.0, 6.0, ((0, 8), (2, 64)), jnp.float32),
        "conv_weight": scatter_about(keys[3], (KERNEL, INNER), KERNEL ** -0.5, 3.0, ((1, 64),), jnp.float32),
        "conv_bias": scatter_about(keys[4], (INNER,), 0.5, 3.0, ((0, 64),), jnp.float32),
        "x_proj": scatter_about(keys[5], (INNER, DT_RANK + 2 * STATE), INNER ** -0.5, 0.046875, ((0, 64),)),
        "dt_norm_gain": jnp.clip(1.0 + 0.18 * jax.random.normal(keys[6], (DT_RANK,), jnp.float32), 0.1, 1.9),
        "dt_proj": scatter_about(keys[7], (DT_RANK, INNER), DT_RANK ** -0.5, 0.25, ((1, 64),)),
        "dt_bias": jnp.clip(-2.0 + 3.0 * jax.random.uniform(keys[8], (INNER,), jnp.float32) ** level_of(keys[8], (INNER,), ((0, 64),), -0.2, 0.2), -2.0, 1.0),
        "a_log": jnp.clip(-3.0 + 5.5 * jax.random.uniform(keys[9], (STATE, INNER), jnp.float32) ** level_of(keys[9], (STATE, INNER), ((1, 64),), -0.2, 0.2), -3.0, 2.5),
        "d_skip": jnp.clip(0.5 + 1.0 * jax.random.uniform(keys[10], (INNER,), jnp.float32) ** level_of(keys[10], (INNER,), ((0, 64),), -0.2, 0.2), 0.5, 1.5),
        "query": draw_query(jax.random.fold_in(keys[16], 71), 0),
        "new_kv": draw_new_kv(jax.random.fold_in(keys[16], 71), 0),
        "kv_pool": draw_kv_pool(jax.random.fold_in(keys[16], 71), 0),
        "page_sel": draw_page_sel(jax.random.fold_in(keys[16], 71), 0),
        "lengths": draw_lengths(jax.random.fold_in(keys[16], 71), 0),
    }


epsilon = 1e-06
far_below = -1e+30

def finish_mamba(projected, mixed_bf, gating, ssm_state, dt_norm_gain, dt_proj, dt_bias, a_log, d_skip):
    dt_low = projected[:, :DT_RANK]
    b_terms = projected[:, DT_RANK:DT_RANK + STATE]
    c_terms = projected[:, DT_RANK + STATE:DT_RANK + 2 * STATE]
    inv_rms = lax.rsqrt(lax.optimization_barrier(jnp.mean(dt_low * dt_low, axis=1, keepdims=True)) + epsilon)
    normed = (dt_low * inv_rms * dt_norm_gain[None, :]).astype(jnp.bfloat16)
    step_size = jax.nn.softplus(jnp.dot(normed, dt_proj, preferred_element_type=jnp.float32) + dt_bias[None, :])
    mixed_f = mixed_bf.astype(jnp.float32)
    decay_rate = jnp.exp(step_size[:, None, :] * (-jnp.exp(a_log))[None, :, :])
    new_state = decay_rate * ssm_state + (step_size * mixed_f)[:, None, :] * b_terms[:, :, None]
    readout = lax.optimization_barrier(jnp.sum(c_terms[:, :, None] * new_state, axis=1)) + d_skip[None, :] * mixed_f
    mamba_out = (readout * jax.nn.silu(gating)).astype(jnp.bfloat16)
    return (mamba_out, new_state)

def reference(xz, conv_state, ssm_state, conv_weight, conv_bias, x_proj, dt_norm_gain, dt_proj, dt_bias, a_log, d_skip, query, new_kv, kv_pool, page_sel, lengths):
    inputs = xz[:, 0, :].astype(jnp.float32)
    gating = xz[:, 1, :].astype(jnp.float32)
    window = jnp.concatenate([conv_state.astype(jnp.float32), inputs[:, None, :]], axis=1)
    convolved = lax.optimization_barrier(jnp.sum(window * conv_weight[None, :, :], axis=1)) + conv_bias[None, :]
    mixed_bf = jax.nn.silu(convolved).astype(jnp.bfloat16)
    projected = jnp.dot(mixed_bf, x_proj, preferred_element_type=jnp.float32)
    mamba_out, new_state = finish_mamba(projected, mixed_bf, gating, ssm_state, dt_norm_gain, dt_proj, dt_bias, a_log, d_skip)
    per_group = Q_HEADS // KV_HEADS
    score_scale = 1.0 / math.sqrt(HEAD_DIM)
    group_ids = jnp.arange(NREQ, dtype=jnp.int32) // (REQ_ROWS * TOPK)

    def attend_one(request_args):
        query_row, fresh_row, listed, length, group_id = request_args
        page_rows = (group_id * (TOPK * POOL) + listed).astype(jnp.int32)
        fetched = jnp.take(kv_pool, page_rows, axis=0).reshape(TOPK * PAGE, KV_HEADS, 2, HEAD_DIM).astype(jnp.float32)
        page_keys = fetched[:, :, 0, :]
        page_values = fetched[:, :, 1, :]
        query_heads = query_row.reshape(KV_HEADS, per_group, HEAD_DIM).astype(jnp.float32)
        fresh_kv = fresh_row.reshape(KV_HEADS, 2, HEAD_DIM).astype(jnp.float32)
        scores = jnp.einsum('hgd,khd->hgk', query_heads, page_keys, precision=lax.Precision.HIGHEST) * score_scale
        own_score = jnp.einsum('hgd,hd->hg', query_heads, fresh_kv[:, 0, :], precision=lax.Precision.HIGHEST) * score_scale
        position = jnp.arange(TOPK * PAGE, dtype=jnp.int32)
        usable = (position >= PAGE) | (position < length)
        masked = jnp.where(usable[None, None, :], scores, far_below)
        row_top = jnp.maximum(lax.optimization_barrier(jnp.max(masked, axis=2)), own_score)
        weights = jnp.where(usable[None, None, :], jnp.exp(masked - row_top[:, :, None]), 0.0)
        own_weight = jnp.exp(own_score - row_top)
        row_total = lax.optimization_barrier(jnp.sum(weights, axis=2)) + own_weight
        summed = jnp.einsum('hgk,khd->hgd', weights, page_values, precision=lax.Precision.HIGHEST)
        summed = summed + own_weight[:, :, None] * fresh_kv[:, None, 1, :]
        return (summed / row_total[:, :, None]).reshape(Q_HEADS * HEAD_DIM).astype(jnp.bfloat16)
    attention_out = lax.map(attend_one, (query, new_kv, page_sel, lengths, group_ids))
    return (mamba_out, new_state, attention_out)
```

```python
import functools
import math

import jax
import jax.numpy as jnp
from jax import lax
from jax.experimental import pallas as pl
from jax.experimental.pallas import tpu as pltpu
from jax.sharding import PartitionSpec as P

MESH = pl.DeviceIdType.MESH
STATE = 16
DT_RANK = 512
Q_HEADS = 64
KV_HEADS = 8
HEAD_DIM = 128
PAGE = 64
NZ = 16
NY = 4
POOL = 20
TOPK = 16
EPS = 1e-06
FAR_BELOW = -1e30
FLOOR = -1e29
F32 = jnp.float32
BF16 = jnp.bfloat16

Z_ORDER = (8, 7, 9, 6, 10, 5, 11, 4, 12, 3, 13, 2, 14, 1, 15)
SCALE2 = math.log2(math.e) / math.sqrt(HEAD_DIM)


def silu(v):
    return v / (1.0 + jnp.exp(-v))


def split3(v):
    hi = v.astype(BF16).astype(F32)
    rest = v - hi
    mid = rest.astype(BF16).astype(F32)
    return hi, mid, rest - mid


def kernel(
    xz_h, cs_h, ssm_h, cw_h, cb_h, xp_h, gain_h, dtp_h, dtb_h, alog_h, dskip_h,
    q_h, nkv_h, pool_h, sel_h, len_h,
    mamba_h, state_h, attn_h,
    xz_v, cs_v, ssm_v, cw_v, cb_v, xp_v, gain_v, dtp_v, dtb_v, alog_v, dskip_v,
    q_v, nkv_v, pool_v, sel_s, len_s,
    mamba_v, state_v, attn_v,
    q_all, q_own, cnt_send, cnt_all, scores,
    y_send, y_recv, z_send, z_recv, g_recv, p_send, p_recv, yout,
    load_sem, out_sem,
    q_ss, q_rs, c_ss, c_rs, y_ss, y_rs, z_ss, z_rs, g_ss, g_rs, p_ss, p_rs,
):
    r = lax.axis_index("req")
    h = lax.axis_index("head")
    c = lax.axis_index("ctx")

    def zpeer(i):
        return (r, h, lax.rem(c + i, NZ))

    def ypeer(i):
        return (r, lax.rem(h + i, NY), c)

    barrier = pltpu.get_barrier_semaphore()
    for i in Z_ORDER:
        pl.semaphore_signal(barrier, inc=1, device_id=zpeer(i), device_id_type=MESH)
    for i in range(1, NY):
        pl.semaphore_signal(barrier, inc=1, device_id=ypeer(i), device_id_type=MESH)

    pairs = (
        (q_h, q_v), (sel_h, sel_s), (len_h, len_s), (xz_h, xz_v), (cs_h, cs_v), (cw_h, cw_v), (cb_h, cb_v),
        (xp_h, xp_v), (nkv_h, nkv_v), (pool_h, pool_v), (dtp_h, dtp_v), (gain_h, gain_v),
        (dtb_h, dtb_v), (alog_h, alog_v), (dskip_h, dskip_v), (ssm_h, ssm_v),
    )
    loads = [pltpu.make_async_copy(a, b, load_sem.at[k]) for k, (a, b) in enumerate(pairs)]
    for cp in loads:
        cp.start()

    loads[0].wait()
    qrow = q_v[0:1, :].astype(F32)
    for k in range(16):
        q_own[k : k + 1, :] = qrow[:, k * HEAD_DIM : (k + 1) * HEAD_DIM]
    q_all[c] = q_own[...].astype(BF16)

    loads[1].wait()
    loads[2].wait()
    shard_id = lax.broadcasted_iota(jnp.int32, (NZ, 128), 0)
    slot_id = lax.broadcasted_iota(jnp.int32, (NZ, 128), 1)
    entry = jnp.where(slot_id < POOL, shard_id * POOL + slot_id, -1)
    count = jnp.zeros((NZ, 128), jnp.int32)
    for k in range(TOPK):
        amount = len_s[0, 0] if k == 0 else PAGE
        count = jnp.where(entry == sel_s[0, k], amount, count)
    cnt_send[:, 0, :] = count.astype(F32)
    cnt_all[c] = cnt_send[c]

    for k in (3, 4, 5, 6):
        loads[k].wait()
    conv = cb_v[0:1, :] + cw_v[3:4, :] * xz_v[:, 0, :].astype(F32)
    for k in range(3):
        conv = conv + cw_v[k : k + 1, :] * cs_v[k].astype(F32)
    mixed_bf = silu(conv).astype(BF16)
    loads[7].wait()
    nt = (((1,), (1,)), ((), ()))
    for j in range(5):
        rows = 128 if j < 4 else 2 * STATE
        part = lax.dot_general(mixed_bf, xp_v[j * 128 : j * 128 + rows, :], nt, preferred_element_type=F32)
        if j == 4:
            part = jnp.concatenate([part, jnp.zeros((16, 128 - rows), F32)], axis=1)
        for k in range(NY):
            y_send[k, j] = part[4 * k : 4 * k + 4, :]

    pl.semaphore_wait(barrier, NZ - 1 + NY - 1)

    def remote(src, dst, ss, rs, k, dev):
        cp = pltpu.make_async_remote_copy(
            src_ref=src, dst_ref=dst, send_sem=ss.at[k], recv_sem=rs.at[k], device_id=dev, device_id_type=MESH
        )
        cp.start()
        return cp

    y_cp = [
        remote(y_send.at[lax.rem(h + i, NY)], y_recv.at[i - 1], y_ss, y_rs, i - 1, ypeer(i)) for i in range(1, NY)
    ]
    q_cp = [remote(q_all.at[c], q_all.at[c], q_ss, q_rs, i - 1, zpeer(i)) for i in Z_ORDER]
    c_cp = [
        remote(cnt_send.at[lax.rem(c + i, NZ)], cnt_all.at[c], c_ss, c_rs, i - 1, zpeer(i)) for i in Z_ORDER
    ]

    loads[8].wait()
    nkv = nkv_v[0:1, :].astype(F32)
    half = lax.broadcasted_iota(jnp.int32, (16, HEAD_DIM), 0) < 8
    own_key = jnp.where(half, nkv[:, 0:128], nkv[:, 256:384])
    own_value = jnp.where(half, nkv[:, 128:256], nkv[:, 384:512])
    own_score = jnp.sum(q_own[...] * own_key, axis=1, keepdims=True) * SCALE2
    tokens = POOL * PAGE
    spread = (
        lax.broadcasted_iota(jnp.int32, (128, tokens), 0)
        == lax.broadcasted_iota(jnp.int32, (128, tokens), 1) // PAGE
    ).astype(BF16)
    token_id = lax.rem(lax.broadcasted_iota(jnp.int32, (1, tokens), 1), PAGE).astype(F32)
    for k in range(9, 16):
        loads[k].wait()

    total = y_send[h]
    for i in range(NY - 1):
        y_cp[i].wait_recv()
        total = total + y_recv[i]
    z_send[...] = total
    z_cp = [remote(z_send, z_recv.at[i - 1], z_ss, z_rs, i - 1, zpeer(i)) for i in Z_ORDER]

    for cp in q_cp:
        cp.wait_recv()
    for cp in c_cp:
        cp.wait_recv()
    counts = cnt_all[:, 0, :].astype(BF16)
    limit = jnp.dot(counts, spread, preferred_element_type=F32)
    bias = jnp.where(token_id < limit, 0.0, FAR_BELOW)
    queries = q_all[...].astype(F32)
    lane = lax.broadcasted_iota(jnp.int32, (NZ, 8, HEAD_DIM), 2)
    for v in range(2):
        qv = queries[:, 8 * v : 8 * v + 8, :].reshape(NZ * 8, HEAD_DIM).astype(BF16)
        keys = pool_v[:, :, 256 * v : 256 * v + 128].reshape(tokens, HEAD_DIM)
        values = pool_v[:, :, 256 * v + 128 : 256 * v + 256].reshape(tokens, HEAD_DIM)
        s = lax.dot_general(qv, keys, nt, preferred_element_type=F32) * SCALE2
        s = s.reshape(NZ, 8, tokens) + bias[:, None, :]
        top = jnp.maximum(jnp.max(s, axis=2, keepdims=True), FLOOR)
        w = jnp.exp2(s - top).astype(BF16)
        weight_sum = jnp.sum(w.astype(F32), axis=2, keepdims=True)
        o = jnp.dot(w.reshape(NZ * 8, tokens), values, preferred_element_type=F32).reshape(NZ, 8, HEAD_DIM)
        kept = jnp.maximum(weight_sum, 1.0)
        o = o / kept
        lse = top + jnp.log2(kept)
        hi, mid, low = split3(lse)
        stat = jnp.where(lane == 0, hi, jnp.where(lane == 1, mid, jnp.where(lane == 2, low, 0.0)))
        scores[0, :, 8 * v : 8 * v + 8, :] = o
        scores[1, :, 8 * v : 8 * v + 8, :] = stat
    p_send[:, 0:16, :] = scores[0].astype(BF16)
    p_send[:, 16:32, :] = scores[1].astype(BF16)
    p_cp = [
        remote(p_send.at[lax.rem(c + i, NZ)], p_recv.at[i - 1], p_ss, p_rs, i - 1, zpeer(i)) for i in Z_ORDER
    ]

    total = z_send[...]
    for cp in z_cp:
        cp.wait_recv()
    for i in range(NZ - 1):
        total = total + z_recv[i]
    low_part = total[0:4]
    square = jnp.sum(jnp.sum(low_part * low_part, axis=0), axis=1, keepdims=True) * (1.0 / DT_RANK)
    inv = lax.rsqrt(square + EPS)
    for j in range(4):
        g_recv[h, j] = total[j] * inv * gain_v[0:1, j * 128 : (j + 1) * 128]
    g_recv[h, 4] = total[4]
    g_cp = [remote(g_recv.at[h], g_recv.at[h], g_ss, g_rs, i - 1, ypeer(i)) for i in range(1, NY)]
    rate = jnp.exp(alog_v[...])
    gate = silu(xz_v[:, 1, :].astype(F32))
    mixed = mixed_bf.astype(F32)
    for cp in g_cp:
        cp.wait_recv()

    step = dtb_v[0:1, :]
    for j in range(4):
        normed = jnp.concatenate([g_recv[k, j] for k in range(NY)], axis=0).astype(BF16)
        step = step + jnp.dot(normed, dtp_v[j * 128 : (j + 1) * 128, :], preferred_element_type=F32)
    step = jnp.maximum(step, 0.0) + jnp.log1p(jnp.exp(-jnp.abs(step)))
    terms = jnp.concatenate([g_recv[k, 4] for k in range(NY)] + [jnp.zeros((112, 128), F32)], axis=0).T
    drive = step * mixed
    for i in range(16):
        decay = jnp.exp(-(step[i : i + 1, :] * rate))
        new = decay * ssm_v[i] + drive[i : i + 1, :] * terms[0:16, i : i + 1]
        state_v[i] = new
        yout[i : i + 1, :] = jnp.sum(terms[16:32, i : i + 1] * new, axis=0, keepdims=True)
    out_state = pltpu.make_async_copy(state_v, state_h, out_sem.at[0])
    out_state.start()
    mamba_v[...] = ((yout[...] + dskip_v[0:1, :] * mixed) * gate).astype(BF16)
    out_mamba = pltpu.make_async_copy(mamba_v, mamba_h, out_sem.at[1])
    out_mamba.start()

    for cp in p_cp:
        cp.wait_recv()
    parts = [p_send[c]] + [p_recv[i] for i in range(NZ - 1)]
    levels = [jnp.sum(x[16:32, :].astype(F32), axis=1, keepdims=True) for x in parts]
    top = own_score
    for x in levels:
        top = jnp.maximum(top, x)
    weight = jnp.exp2(own_score - top)
    summed = weight * own_value
    for x, level in zip(parts, levels):
        w = jnp.exp2(level - top)
        summed = summed + w * x[0:16, :].astype(F32)
        weight = weight + w
    attn_v[...] = (summed / weight).astype(BF16)
    out_attn = pltpu.make_async_copy(attn_v, attn_h, out_sem.at[2])
    out_attn.start()

    for cp in y_cp + q_cp + c_cp + z_cp + g_cp + p_cp:
        cp.wait_send()
    out_state.wait()
    out_mamba.wait()
    out_attn.wait()


def on_device(
    xz, conv_state, ssm_state, conv_weight, conv_bias, x_proj, dt_norm_gain, dt_proj, dt_bias, a_log, d_skip,
    query, new_kv, kv_pool, page_sel, lengths,
):
    args = (
        xz, conv_state.transpose(1, 0, 2), ssm_state, conv_weight, conv_bias.reshape(1, -1), x_proj.T,
        dt_norm_gain.reshape(1, -1), dt_proj, dt_bias.reshape(1, -1), a_log, d_skip.reshape(1, -1),
        query, new_kv, kv_pool, page_sel, lengths.reshape(1, 1),
    )
    hbm = pl.BlockSpec(memory_space=pltpu.HBM)
    outs = (
        jax.ShapeDtypeStruct((16, 256), BF16),
        jax.ShapeDtypeStruct((16, STATE, 256), F32),
        jax.ShapeDtypeStruct((16, HEAD_DIM), BF16),
    )
    in_smem = {14, 15}
    scratch = [
        (pltpu.SMEM if k in in_smem else pltpu.VMEM)(a.shape, a.dtype) for k, a in enumerate(args)
    ]
    scratch += [pltpu.VMEM(o.shape, o.dtype) for o in outs]
    scratch += [
        pltpu.VMEM((NZ, 16, HEAD_DIM), BF16),
        pltpu.VMEM((16, HEAD_DIM), F32),
        pltpu.VMEM((NZ, 1, 128), F32),
        pltpu.VMEM((NZ, 1, 128), F32),
        pltpu.VMEM((2, NZ, 16, HEAD_DIM), F32),
        pltpu.VMEM((NY, 5, 4, 128), F32),
        pltpu.VMEM((NY - 1, 5, 4, 128), F32),
        pltpu.VMEM((5, 4, 128), F32),
        pltpu.VMEM((NZ - 1, 5, 4, 128), F32),
        pltpu.VMEM((NY, 5, 4, 128), F32),
        pltpu.VMEM((NZ, 32, HEAD_DIM), BF16),
        pltpu.VMEM((NZ - 1, 32, HEAD_DIM), BF16),
        pltpu.VMEM((16, 256), F32),
        pltpu.SemaphoreType.DMA((len(args),)),
        pltpu.SemaphoreType.DMA((3,)),
    ]
    for n in (NZ - 1, NZ - 1, NY - 1, NZ - 1, NY - 1, NZ - 1):
        scratch += [pltpu.SemaphoreType.DMA((n,)), pltpu.SemaphoreType.DMA((n,))]
    mamba_out, new_state, attention = pl.pallas_call(
        kernel,
        out_shape=outs,
        in_specs=[hbm] * len(args),
        out_specs=[hbm] * 3,
        scratch_shapes=scratch,
        name="decode_step",
        compiler_params=pltpu.CompilerParams(
            collective_id=0, has_side_effects=True, vmem_limit_bytes=40 * 2**20
        ),
    )(*args)
    return mamba_out, new_state, attention.reshape(1, 16 * HEAD_DIM)


def solution(mesh):
    placed = (
        P("req", None, ("head", "ctx")),
        P("req", None, ("head", "ctx")),
        P("req", None, ("head", "ctx")),
        P(None, ("head", "ctx")),
        P(("head", "ctx")),
        P(("head", "ctx"), None),
        P(),
        P(None, ("head", "ctx")),
        P(("head", "ctx")),
        P(None, ("head", "ctx")),
        P(("head", "ctx")),
        P(("req", "ctx"), "head"),
        P(("req", "ctx"), "head"),
        P(("req", "ctx"), None, "head"),
        P(("req", "ctx"), None),
        P(("req", "ctx")),
    )
    return jax.shard_map(
        on_device,
        mesh=mesh,
        in_specs=placed,
        out_specs=(
            P("req", ("head", "ctx")),
            P("req", None, ("head", "ctx")),
            P(("req", "ctx"), "head"),
        ),
        check_vma=False,
    )
```

```python
import functools
import math

import jax
import jax.numpy as jnp
from jax import lax
from jax.experimental import pallas as pl
from jax.experimental.pallas import tpu as pltpu
from jax.sharding import PartitionSpec as P

MESH = pl.DeviceIdType.MESH
STATE = 16
DT_RANK = 512
Q_HEADS = 64
KV_HEADS = 8
HEAD_DIM = 128
PAGE = 64
NZ = 16
NY = 4
POOL = 20
TOPK = 16
EPS = 1e-06
FAR_BELOW = -1e30
FLOOR = -1e29
F32 = jnp.float32
BF16 = jnp.bfloat16

SLOTS = (0, 1, 15, 2, 14, 3, 13, 4, 12, 5, 11, 6, 10, 7, 9, 8)
SLOT_OF = {i: k for k, i in enumerate(SLOTS)}
FAR_FIRST = SLOTS[:0:-1]
GROUPS = ((0, 8), (8, 16))
SCALE2 = math.log2(math.e) / math.sqrt(HEAD_DIM)
NT = (((1,), (1,)), ((), ()))


def silu(v):
    return v / (1.0 + jnp.exp(-v))


def kernel(
    xz_h, cs_h, ssm_h, cw_h, cb_h, xp_h, gain_h, dtp_h, dtb_h, alog_h, dskip_h,
    q_h, nkv_h, pool_h, sel_h, len_h,
    mamba_v, state_v, attn_v,
    xz_v, cs_v, ssm_v, cw_v, cb_v, xp_v, gain_v, dtp_v, dtb_v, alog_v, dskip_v,
    q_v, nkv_v, pool_v, sel_s, len_s,
    q_own, q_all, cnt_send, cnt_all, y_send, y_recv, z_send, zb_send, z_recv, zb_recv, g_recv,
    p_send, pl_send, p_recv, pl_recv, yout,
    load_sem, q_ss, q_rs, c_ss, c_rs, y_ss, y_rs, z_ss, z_rs, zb_ss, zb_rs, g_ss, g_rs, p_ss, p_rs, pl_ss, pl_rs,
):
    r = lax.axis_index("req")
    h = lax.axis_index("head")
    c = lax.axis_index("ctx")

    def zpeer(i):
        return (r, h, lax.rem(c + i, NZ))

    def ypeer(i):
        return (r, lax.rem(h + i, NY), c)

    started = []

    def remote(src, dst, ss, rs, k, dev):
        cp = pltpu.make_async_remote_copy(
            src_ref=src, dst_ref=dst, send_sem=ss.at[k], recv_sem=rs.at[k], device_id=dev, device_id_type=MESH
        )
        cp.start()
        started.append(cp)
        return cp

    barrier = pltpu.get_barrier_semaphore()
    for i in FAR_FIRST:
        pl.semaphore_signal(barrier, inc=1, device_id=zpeer(i), device_id_type=MESH)
    for i in range(1, NY):
        pl.semaphore_signal(barrier, inc=1, device_id=ypeer(i), device_id_type=MESH)

    pairs = (
        (q_h, q_v), (sel_h, sel_s), (len_h, len_s), (xz_h, xz_v), (cs_h, cs_v), (cw_h, cw_v), (cb_h, cb_v),
        (xp_h, xp_v), (nkv_h, nkv_v), (pool_h, pool_v), (dtp_h, dtp_v), (gain_h, gain_v),
        (dtb_h, dtb_v), (alog_h, alog_v), (dskip_h, dskip_v), (ssm_h, ssm_v),
    )
    loads = [pltpu.make_async_copy(a, b, load_sem.at[k]) for k, (a, b) in enumerate(pairs)]
    for cp in loads:
        cp.start()

    loads[0].wait()
    qrow = q_v[0:1, :].astype(F32)
    for k in range(16):
        q_own[k : k + 1, :] = qrow[:, k * HEAD_DIM : (k + 1) * HEAD_DIM]
    q_all[0] = q_own[...].astype(BF16)

    loads[1].wait()
    loads[2].wait()
    shard_id = lax.broadcasted_iota(jnp.int32, (NZ, 128), 0)
    slot_id = lax.broadcasted_iota(jnp.int32, (NZ, 128), 1)
    entry = jnp.where(slot_id < POOL, shard_id * POOL + slot_id, -1)
    count = jnp.zeros((NZ, 128), jnp.int32)
    for k in range(TOPK):
        amount = len_s[0, 0] if k == 0 else PAGE
        count = jnp.where(entry == sel_s[0, k], amount, count)
    cnt_send[:, 0, :] = count.astype(F32)
    cnt_all[0] = cnt_send[c]

    for k in (3, 4, 5, 6):
        loads[k].wait()
    conv = cb_v[0:1, :] + cw_v[3:4, :] * xz_v[:, 0, :].astype(F32)
    for k in range(3):
        conv = conv + cw_v[k : k + 1, :] * cs_v[k].astype(F32)
    mixed_bf = silu(conv).astype(BF16)
    loads[7].wait()
    for j in range(4):
        part = lax.dot_general(mixed_bf, xp_v[j * 128 : (j + 1) * 128, :], NT, preferred_element_type=F32)
        for k in range(NY):
            y_send[k, 4 * j : 4 * j + 4, :] = part[4 * k : 4 * k + 4, :]
    part = lax.dot_general(mixed_bf, xp_v[DT_RANK : DT_RANK + 32, :], NT, preferred_element_type=F32)
    for k in range(NY):
        y_send[k, 16:17, :] = jnp.concatenate([part[4 * k + i : 4 * k + i + 1, :] for i in range(4)], axis=1)

    pl.semaphore_wait(barrier, NZ - 1 + NY - 1)

    y_cp = [
        remote(y_send.at[lax.rem(h + i, NY)], y_recv.at[i - 1], y_ss, y_rs, i - 1, ypeer(i)) for i in range(1, NY)
    ]
    q_cp, c_cp = {}, {}
    for i in FAR_FIRST:
        q_cp[i] = remote(q_all.at[0], q_all.at[SLOT_OF[i]], q_ss, q_rs, i - 1, zpeer(i))
        c_cp[i] = remote(
            cnt_send.at[lax.rem(c + i, NZ)], cnt_all.at[SLOT_OF[i]], c_ss, c_rs, i - 1, zpeer(i)
        )

    loads[8].wait()
    nkv = nkv_v[0:1, :].astype(F32)
    half = lax.broadcasted_iota(jnp.int32, (16, HEAD_DIM), 0) < 8
    own_key = jnp.where(half, nkv[:, 0:128], nkv[:, 256:384])
    own_value = jnp.where(half, nkv[:, 128:256], nkv[:, 384:512])
    own_score = jnp.sum(q_own[...] * own_key, axis=1, keepdims=True) * SCALE2
    tokens = POOL * PAGE
    spread = (
        lax.broadcasted_iota(jnp.int32, (128, tokens), 0)
        == lax.broadcasted_iota(jnp.int32, (128, tokens), 1) // PAGE
    ).astype(BF16)
    token_id = lax.rem(lax.broadcasted_iota(jnp.int32, (1, tokens), 1), PAGE).astype(F32)
    for k in range(9, 16):
        loads[k].wait()
    gain = jnp.concatenate(
        [jnp.broadcast_to(gain_v[0:1, j * 128 : (j + 1) * 128], (4, 128)) for j in range(4)], axis=0
    )

    total = y_send[h]
    for i in range(NY - 1):
        y_cp[i].wait_recv()
        total = total + y_recv[i]
    z_send[...] = total[0:16].astype(BF16)
    zb_send[...] = total[16:17]
    z_cp, zb_cp = {}, {}
    for i in FAR_FIRST:
        z_cp[i] = remote(z_send, z_recv.at[i - 1], z_ss, z_rs, i - 1, zpeer(i))
        zb_cp[i] = remote(zb_send, zb_recv.at[i - 1], zb_ss, zb_rs, i - 1, zpeer(i))

    diagonal = (
        lax.broadcasted_iota(jnp.int32, (1, 16, HEAD_DIM), 1)
        == lax.broadcasted_iota(jnp.int32, (1, 16, HEAD_DIM), 2)
    )
    p_cp, pl_cp = {}, {}
    for first, last in GROUPS:
        n = last - first
        for i in SLOTS[first:last]:
            if i:
                c_cp[i].wait_recv()
                q_cp[i].wait_recv()
        counts = cnt_all[first:last, 0, :].astype(BF16)
        limit = jnp.dot(counts, spread, preferred_element_type=F32)
        bias = jnp.where(token_id < limit, 0.0, FAR_BELOW)
        queries = q_all[first:last].astype(F32)
        outs, levels = [], []
        for v in range(2):
            qv = queries[:, 8 * v : 8 * v + 8, :].reshape(n * 8, HEAD_DIM).astype(BF16)
            keys = pool_v[:, :, 256 * v : 256 * v + 128].reshape(tokens, HEAD_DIM)
            values = pool_v[:, :, 256 * v + 128 : 256 * v + 256].reshape(tokens, HEAD_DIM)
            s = lax.dot_general(qv, keys, NT, preferred_element_type=F32) * SCALE2
            s = s.reshape(n, 8, tokens) + bias[:, None, :]
            top = jnp.maximum(jnp.max(s, axis=2, keepdims=True), FLOOR)
            w = jnp.exp2(s - top).astype(BF16)
            weight_sum = jnp.sum(w.astype(F32), axis=2, keepdims=True)
            o = jnp.dot(w.reshape(n * 8, tokens), values, preferred_element_type=F32).reshape(n, 8, HEAD_DIM)
            kept = jnp.maximum(weight_sum, 1.0)
            outs.append(o / kept)
            levels.append(top + jnp.log2(kept))
        level = jnp.concatenate(levels, axis=1)
        p_send[first:last] = jnp.concatenate(outs, axis=1).astype(BF16)
        pl_send[first:last] = jnp.sum(jnp.where(diagonal, level, 0.0), axis=1, keepdims=True)
        for i in SLOTS[first:last][::-1]:
            if i:
                k = SLOT_OF[i]
                back = NZ - i
                p_cp[back] = remote(p_send.at[k], p_recv.at[SLOT_OF[back]], p_ss, p_rs, back - 1, zpeer(back))
                pl_cp[back] = remote(pl_send.at[k], pl_recv.at[SLOT_OF[back]], pl_ss, pl_rs, back - 1, zpeer(back))

    total = total[0:16]
    terms = zb_send[...]
    for i in SLOTS[1:]:
        z_cp[i].wait_recv()
        zb_cp[i].wait_recv()
        total = total + z_recv[i - 1].astype(F32)
        terms = terms + zb_recv[i - 1]
    square = total * total
    square = square[0:8] + square[8:16]
    square = square + jnp.concatenate([square[4:8], square[0:4]], axis=0)
    square = jnp.sum(square, axis=1, keepdims=True) * (1.0 / DT_RANK)
    inv = lax.rsqrt(square + EPS)
    g_recv[h, 0:16, :] = total * jnp.concatenate([inv, inv], axis=0) * gain
    g_recv[h, 16:17, :] = terms
    g_cp = [remote(g_recv.at[h], g_recv.at[h], g_ss, g_rs, i - 1, ypeer(i)) for i in range(1, NY)]
    rate = jnp.exp(alog_v[...])
    gate = silu(xz_v[:, 1, :].astype(F32))
    mixed = mixed_bf.astype(F32)
    for cp in g_cp:
        cp.wait_recv()

    step = dtb_v[0:1, :]
    for j in range(4):
        normed = jnp.concatenate([g_recv[k, 4 * j : 4 * j + 4, :] for k in range(NY)], axis=0).astype(BF16)
        step = step + jnp.dot(normed, dtp_v[j * 128 : (j + 1) * 128, :], preferred_element_type=F32)
    step = jnp.maximum(step, 0.0) + jnp.log1p(jnp.exp(-jnp.abs(step)))
    terms = jnp.concatenate([g_recv[k, 16:17, :] for k in range(NY)] + [jnp.zeros((124, 128), F32)], axis=0).T
    drive = step * mixed
    for i in range(16):
        k, low = i // 4, 32 * (i % 4)
        decay = jnp.exp(-(step[i : i + 1, :] * rate))
        new = decay * ssm_v[i] + drive[i : i + 1, :] * terms[low : low + 16, k : k + 1]
        state_v[i] = new
        yout[i : i + 1, :] = jnp.sum(terms[low + 16 : low + 32, k : k + 1] * new, axis=0, keepdims=True)
    mamba_v[...] = ((yout[...] + dskip_v[0:1, :] * mixed) * gate).astype(BF16)

    p_recv[0] = p_send[0]
    pl_recv[0] = pl_send[0]
    top, weight, summed = own_score, jnp.ones_like(own_score), own_value
    for first, last in GROUPS:
        for i in SLOTS[first:last]:
            if i:
                pl_cp[i].wait_recv()
                p_cp[i].wait_recv()
        level = jnp.sum(jnp.where(diagonal, pl_recv[first:last], 0.0), axis=2, keepdims=True)
        new_top = jnp.maximum(top, jnp.max(level, axis=0))
        old = jnp.exp2(top - new_top)
        w = jnp.exp2(level - new_top[None])
        weight = weight * old + jnp.sum(w, axis=0)
        summed = summed * old + jnp.sum(w * p_recv[first:last].astype(F32), axis=0)
        top = new_top
    joined = (summed / weight).astype(BF16)
    for k in range(16):
        attn_v[0:1, k * HEAD_DIM : (k + 1) * HEAD_DIM] = joined[k : k + 1, :]

    for cp in started:
        cp.wait_send()


def hand_over(a_in, b_in, c_in, a_out, b_out, c_out, sem):
    copies = [
        pltpu.make_async_copy(x, y, sem.at[k])
        for k, (x, y) in enumerate(((a_in, a_out), (b_in, b_out), (c_in, c_out)))
    ]
    for cp in copies:
        cp.start()
    for cp in copies:
        cp.wait()


def on_device(
    xz, conv_state, ssm_state, conv_weight, conv_bias, x_proj, dt_norm_gain, dt_proj, dt_bias, a_log, d_skip,
    query, new_kv, kv_pool, page_sel, lengths,
):
    args = (
        xz, conv_state.transpose(1, 0, 2), ssm_state, conv_weight, conv_bias.reshape(1, -1), x_proj.T,
        dt_norm_gain.reshape(1, -1), dt_proj, dt_bias.reshape(1, -1), a_log, d_skip.reshape(1, -1),
        query, new_kv, kv_pool, page_sel, lengths.reshape(1, 1),
    )
    hbm = pl.BlockSpec(memory_space=pltpu.HBM)
    vmem = pl.BlockSpec(memory_space=pltpu.VMEM)
    outs = (((16, 256), BF16), ((16, STATE, 256), F32), ((1, 16 * HEAD_DIM), BF16))
    in_smem = {14, 15}
    scratch = [
        (pltpu.SMEM if k in in_smem else pltpu.VMEM)(a.shape, a.dtype) for k, a in enumerate(args)
    ]
    scratch += [
        pltpu.VMEM((16, HEAD_DIM), F32),
        pltpu.VMEM((NZ, 16, HEAD_DIM), BF16),
        pltpu.VMEM((NZ, 1, 128), F32),
        pltpu.VMEM((NZ, 1, 128), F32),
        pltpu.VMEM((NY, 17, 128), F32),
        pltpu.VMEM((NY - 1, 17, 128), F32),
        pltpu.VMEM((16, 128), BF16),
        pltpu.VMEM((1, 128), F32),
        pltpu.VMEM((NZ - 1, 16, 128), BF16),
        pltpu.VMEM((NZ - 1, 1, 128), F32),
        pltpu.VMEM((NY, 17, 128), F32),
        pltpu.VMEM((NZ, 16, HEAD_DIM), BF16),
        pltpu.VMEM((NZ, 1, 128), F32),
        pltpu.VMEM((NZ, 16, HEAD_DIM), BF16),
        pltpu.VMEM((NZ, 1, 128), F32),
        pltpu.VMEM((16, 256), F32),
        pltpu.SemaphoreType.DMA((len(args),)),
    ]
    for n in (NZ - 1, NZ - 1, NY - 1, NZ - 1, NZ - 1, NY - 1, NZ - 1, NZ - 1):
        scratch += [pltpu.SemaphoreType.DMA((n,)), pltpu.SemaphoreType.DMA((n,))]
    made = pl.pallas_call(
        kernel,
        out_shape=[pltpu.VMEM(*o) for o in outs],
        in_specs=[hbm] * len(args),
        out_specs=[vmem] * 3,
        scratch_shapes=scratch,
        name="decode_step",
        compiler_params=pltpu.CompilerParams(
            collective_id=0, has_side_effects=True, vmem_limit_bytes=60 * 2**20
        ),
    )(*args)
    return pl.pallas_call(
        hand_over,
        out_shape=[jax.ShapeDtypeStruct(*o) for o in outs],
        in_specs=[vmem] * 3,
        out_specs=[hbm] * 3,
        scratch_shapes=[pltpu.SemaphoreType.DMA((3,))],
        name="hand_over",
        compiler_params=pltpu.CompilerParams(vmem_limit_bytes=4 * 2**20),
    )(*made)


def solution(mesh):
    placed = (
        P("req", None, ("head", "ctx")),
        P("req", None, ("head", "ctx")),
        P("req", None, ("head", "ctx")),
        P(None, ("head", "ctx")),
        P(("head", "ctx")),
        P(("head", "ctx"), None),
        P(),
        P(None, ("head", "ctx")),
        P(("head", "ctx")),
        P(None, ("head", "ctx")),
        P(("head", "ctx")),
        P(("req", "ctx"), "head"),
        P(("req", "ctx"), "head"),
        P(("req", "ctx"), None, "head"),
        P(("req", "ctx"), None),
        P(("req", "ctx")),
    )
    return jax.shard_map(
        on_device,
        mesh=mesh,
        in_specs=placed,
        out_specs=(
            P("req", ("head", "ctx")),
            P("req", None, ("head", "ctx")),
            P(("req", "ctx"), "head"),
        ),
        check_vma=False,
    )
```

```python
import functools
import math

import jax
import jax.numpy as jnp
from jax import lax
from jax.experimental import pallas as pl
from jax.experimental.pallas import tpu as pltpu
from jax.sharding import PartitionSpec as P

MESH = pl.DeviceIdType.MESH
STATE = 16
DT_RANK = 512
Q_HEADS = 64
KV_HEADS = 8
HEAD_DIM = 128
PAGE = 64
NZ = 16
NY = 4
POOL = 20
TOPK = 16
EPS = 1e-06
FAR_BELOW = -1e30
FLOOR = -1e29
F32 = jnp.float32
BF16 = jnp.bfloat16

SLOTS = (0, 1, 15, 2, 14, 3, 13, 4, 12, 5, 11, 6, 10, 7, 9, 8)
SLOT_OF = {i: k for k, i in enumerate(SLOTS)}
FAR_FIRST = SLOTS[:0:-1]
GROUPS = ((0, 8), (8, 16))
SCALE2 = math.log2(math.e) / math.sqrt(HEAD_DIM)
NT = (((1,), (1,)), ((), ()))


def silu(v):
    return v / (1.0 + jnp.exp(-v))


def kernel(
    xz_h, cs_h, ssm_h, cw_h, cb_h, xp_h, gain_h, dtp_h, dtb_h, alog_h, dskip_h,
    q_h, nkv_h, pool_h, sel_h, len_h,
    mamba_v, state_v, attn_v,
    xz_v, cs_v, ssm_v, cw_v, cb_v, xp_v, gain_v, dtp_v, dtb_v, alog_v, dskip_v,
    q_v, nkv_v, pool_v, sel_s, len_s,
    q_own, q_all, cnt_send, cnt_all, y_send, y_recv, z_send, zb_send, z_recv, zb_recv, g_recv,
    p_send, pl_send, p_recv, pl_recv, yout,
    load_sem, q_ss, q_rs, c_ss, c_rs, y_ss, y_rs, z_ss, z_rs, zb_ss, zb_rs, g_ss, g_rs, p_ss, p_rs, pl_ss, pl_rs,
):
    r = lax.axis_index("req")
    h = lax.axis_index("head")
    c = lax.axis_index("ctx")

    def zpeer(i):
        return (r, h, lax.rem(c + i, NZ))

    def ypeer(i):
        return (r, lax.rem(h + i, NY), c)

    def send(src, dst, ss, rs, dev):
        pltpu.make_async_remote_copy(
            src_ref=src, dst_ref=dst, send_sem=ss, recv_sem=rs, device_id=dev, device_id_type=MESH
        ).start()

    def drain(ref, sem):
        pltpu.make_async_copy(ref, ref, sem).wait()

    def part_of(first, last):
        return pl.ds(max(first, 1), last - max(first, 1))

    def group_of(i):
        return next(g for g, (first, last) in enumerate(GROUPS) if first <= SLOT_OF[i] < last)

    barrier = pltpu.get_barrier_semaphore()
    for i in FAR_FIRST:
        pl.semaphore_signal(barrier, inc=1, device_id=zpeer(i), device_id_type=MESH)
    for i in range(1, NY):
        pl.semaphore_signal(barrier, inc=1, device_id=ypeer(i), device_id_type=MESH)

    pairs = (
        (q_h, q_v), (sel_h, sel_s), (len_h, len_s), (xz_h, xz_v), (cs_h, cs_v), (cw_h, cw_v), (cb_h, cb_v),
        (xp_h, xp_v), (nkv_h, nkv_v), (pool_h, pool_v), (dtp_h, dtp_v), (gain_h, gain_v),
        (dtb_h, dtb_v), (alog_h, alog_v), (dskip_h, dskip_v), (ssm_h, ssm_v),
    )
    loads = [pltpu.make_async_copy(a, b, load_sem.at[k]) for k, (a, b) in enumerate(pairs)]
    for cp in loads:
        cp.start()

    loads[0].wait()
    qrow = q_v[0:1, :].astype(F32)
    for k in range(16):
        q_own[k : k + 1, :] = qrow[:, k * HEAD_DIM : (k + 1) * HEAD_DIM]
    q_all[0] = q_own[...].astype(BF16)

    loads[1].wait()
    loads[2].wait()
    shard_id = lax.broadcasted_iota(jnp.int32, (NZ, 128), 0)
    slot_id = lax.broadcasted_iota(jnp.int32, (NZ, 128), 1)
    entry = jnp.where(slot_id < POOL, shard_id * POOL + slot_id, -1)
    count = jnp.zeros((NZ, 128), jnp.int32)
    for k in range(TOPK):
        amount = len_s[0, 0] if k == 0 else PAGE
        count = jnp.where(entry == sel_s[0, k], amount, count)
    cnt_send[:, 0, :] = count.astype(F32)
    cnt_all[0] = cnt_send[c]

    for k in (3, 4, 5, 6):
        loads[k].wait()
    conv = cb_v[0:1, :] + cw_v[3:4, :] * xz_v[:, 0, :].astype(F32)
    for k in range(3):
        conv = conv + cw_v[k : k + 1, :] * cs_v[k].astype(F32)
    mixed_bf = silu(conv).astype(BF16)
    loads[7].wait()
    for j in range(4):
        part = lax.dot_general(mixed_bf, xp_v[j * 128 : (j + 1) * 128, :], NT, preferred_element_type=F32)
        for k in range(NY):
            y_send[k, 4 * j : 4 * j + 4, :] = part[4 * k : 4 * k + 4, :]
    part = lax.dot_general(mixed_bf, xp_v[DT_RANK : DT_RANK + 32, :], NT, preferred_element_type=F32)
    for k in range(NY):
        y_send[k, 16:17, :] = jnp.concatenate([part[4 * k + i : 4 * k + i + 1, :] for i in range(4)], axis=1)

    loads[8].wait()
    nkv = nkv_v[0:1, :].astype(F32)
    half = lax.broadcasted_iota(jnp.int32, (16, HEAD_DIM), 0) < 8
    own_key = jnp.where(half, nkv[:, 0:128], nkv[:, 256:384])
    own_value = jnp.where(half, nkv[:, 128:256], nkv[:, 384:512])
    own_score = jnp.sum(q_own[...] * own_key, axis=1, keepdims=True) * SCALE2
    tokens = POOL * PAGE
    lane = lax.broadcasted_iota(jnp.int32, (1, 128), 1)
    low_half = lane < PAGE
    token = jnp.where(low_half, lane, lane - PAGE).astype(F32)
    for k in range(9, 16):
        loads[k].wait()
    gain = jnp.concatenate(
        [jnp.broadcast_to(gain_v[0:1, j * 128 : (j + 1) * 128], (4, 128)) for j in range(4)], axis=0
    )

    pl.semaphore_wait(barrier, NZ - 1 + NY - 1)

    for i in range(1, NY):
        send(y_send.at[lax.rem(h + i, NY)], y_recv.at[i - 1], y_ss, y_rs, ypeer(i))
    for i in FAR_FIRST:
        g = group_of(i)
        send(q_all.at[0], q_all.at[SLOT_OF[i]], q_ss, q_rs.at[g], zpeer(i))
        send(cnt_send.at[lax.rem(c + i, NZ)], cnt_all.at[SLOT_OF[i]], c_ss, c_rs.at[g], zpeer(i))

    total = y_send[h]
    drain(y_recv, y_rs)
    for i in range(NY - 1):
        total = total + y_recv[i]
    z_send[...] = total[0:16].astype(BF16)
    zb_send[...] = total[16:17]
    for i in FAR_FIRST:
        send(z_send, z_recv.at[i - 1], z_ss, z_rs, zpeer(i))
        send(zb_send, zb_recv.at[i - 1], zb_ss, zb_rs, zpeer(i))

    diagonal = (
        lax.broadcasted_iota(jnp.int32, (1, 16, HEAD_DIM), 1)
        == lax.broadcasted_iota(jnp.int32, (1, 16, HEAD_DIM), 2)
    )
    for g, (first, last) in enumerate(GROUPS):
        n = last - first
        drain(cnt_all.at[part_of(first, last)], c_rs.at[g])
        drain(q_all.at[part_of(first, last)], q_rs.at[g])
        counts = cnt_all[first:last, 0, :]
        bias = jnp.concatenate(
            [
                jnp.where(
                    token < jnp.where(low_half, counts[:, 2 * j : 2 * j + 1], counts[:, 2 * j + 1 : 2 * j + 2]),
                    0.0,
                    FAR_BELOW,
                )
                for j in range(POOL // 2)
            ],
            axis=1,
        )
        queries = q_all[first:last].astype(F32)
        outs, levels = [], []
        for v in range(2):
            qv = queries[:, 8 * v : 8 * v + 8, :].reshape(n * 8, HEAD_DIM).astype(BF16)
            keys = pool_v[:, :, 256 * v : 256 * v + 128].reshape(tokens, HEAD_DIM)
            values = pool_v[:, :, 256 * v + 128 : 256 * v + 256].reshape(tokens, HEAD_DIM)
            s = lax.dot_general(qv, keys, NT, preferred_element_type=F32) * SCALE2
            s = s.reshape(n, 8, tokens) + bias[:, None, :]
            top = jnp.maximum(jnp.max(s, axis=2, keepdims=True), FLOOR)
            w = jnp.exp2(s - top).astype(BF16)
            weight_sum = jnp.sum(w.astype(F32), axis=2, keepdims=True)
            o = jnp.dot(w.reshape(n * 8, tokens), values, preferred_element_type=F32).reshape(n, 8, HEAD_DIM)
            kept = jnp.maximum(weight_sum, 1.0)
            outs.append(o / kept)
            levels.append(top + jnp.log2(kept))
        level = jnp.concatenate(levels, axis=1)
        p_send[first:last] = jnp.concatenate(outs, axis=1).astype(BF16)
        pl_send[first:last] = jnp.sum(jnp.where(diagonal, level, 0.0), axis=1, keepdims=True)
        for i in SLOTS[first:last][::-1]:
            if i:
                k, back = SLOT_OF[i], NZ - i
                slot, to = SLOT_OF[back], group_of(back)
                send(p_send.at[k], p_recv.at[slot], p_ss, p_rs.at[to], zpeer(back))
                send(pl_send.at[k], pl_recv.at[slot], pl_ss, pl_rs.at[to], zpeer(back))

    total = total[0:16]
    terms = zb_send[...]
    drain(z_recv, z_rs)
    drain(zb_recv, zb_rs)
    for i in SLOTS[1:]:
        total = total + z_recv[i - 1].astype(F32)
        terms = terms + zb_recv[i - 1]
    square = total * total
    square = square[0:8] + square[8:16]
    square = square + jnp.concatenate([square[4:8], square[0:4]], axis=0)
    square = jnp.sum(square, axis=1, keepdims=True) * (1.0 / DT_RANK)
    inv = lax.rsqrt(square + EPS)
    g_recv[h, 0:16, :] = total * jnp.concatenate([inv, inv], axis=0) * gain
    g_recv[h, 16:17, :] = terms
    for i in range(1, NY):
        send(g_recv.at[h], g_recv.at[h], g_ss, g_rs, ypeer(i))
    rate = jnp.exp(alog_v[...])
    gate = silu(xz_v[:, 1, :].astype(F32))
    mixed = mixed_bf.astype(F32)
    drain(y_recv, g_rs)

    step = dtb_v[0:1, :]
    for j in range(4):
        normed = jnp.concatenate([g_recv[k, 4 * j : 4 * j + 4, :] for k in range(NY)], axis=0).astype(BF16)
        step = step + jnp.dot(normed, dtp_v[j * 128 : (j + 1) * 128, :], preferred_element_type=F32)
    step = jnp.maximum(step, 0.0) + jnp.log1p(jnp.exp(-jnp.abs(step)))
    terms = jnp.concatenate([g_recv[k, 16:17, :] for k in range(NY)] + [jnp.zeros((124, 128), F32)], axis=0).T
    drive = step * mixed
    for i in range(16):
        k, low = i // 4, 32 * (i % 4)
        decay = jnp.exp(-(step[i : i + 1, :] * rate))
        new = decay * ssm_v[i] + drive[i : i + 1, :] * terms[low : low + 16, k : k + 1]
        state_v[i] = new
        yout[i : i + 1, :] = jnp.sum(terms[low + 16 : low + 32, k : k + 1] * new, axis=0, keepdims=True)
    mamba_v[...] = ((yout[...] + dskip_v[0:1, :] * mixed) * gate).astype(BF16)

    p_recv[0] = p_send[0]
    pl_recv[0] = pl_send[0]
    top, weight, summed = own_score, jnp.ones_like(own_score), own_value
    for g, (first, last) in enumerate(GROUPS):
        drain(pl_recv.at[part_of(first, last)], pl_rs.at[g])
        drain(p_recv.at[part_of(first, last)], p_rs.at[g])
        level = jnp.sum(jnp.where(diagonal, pl_recv[first:last], 0.0), axis=2, keepdims=True)
        new_top = jnp.maximum(top, jnp.max(level, axis=0))
        old = jnp.exp2(top - new_top)
        w = jnp.exp2(level - new_top[None])
        weight = weight * old + jnp.sum(w, axis=0)
        summed = summed * old + jnp.sum(w * p_recv[first:last].astype(F32), axis=0)
        top = new_top
    joined = (summed / weight).astype(BF16)
    for k in range(16):
        attn_v[0:1, k * HEAD_DIM : (k + 1) * HEAD_DIM] = joined[k : k + 1, :]

    peers = pl.ds(1, NZ - 1)
    for ref, sem in (
        (y_recv, y_ss), (q_all.at[peers], q_ss), (cnt_all.at[peers], c_ss), (z_recv, z_ss), (zb_recv, zb_ss),
        (y_recv, g_ss), (p_recv.at[peers], p_ss), (pl_recv.at[peers], pl_ss),
    ):
        drain(ref, sem)


def hand_over(a_in, b_in, c_in, a_out, b_out, c_out, sem):
    copies = [
        pltpu.make_async_copy(x, y, sem.at[k])
        for k, (x, y) in enumerate(((a_in, a_out), (b_in, b_out), (c_in, c_out)))
    ]
    for cp in copies:
        cp.start()
    for cp in copies:
        cp.wait()


def on_device(
    xz, conv_state, ssm_state, conv_weight, conv_bias, x_proj, dt_norm_gain, dt_proj, dt_bias, a_log, d_skip,
    query, new_kv, kv_pool, page_sel, lengths,
):
    args = (
        xz, conv_state.transpose(1, 0, 2), ssm_state, conv_weight, conv_bias.reshape(1, -1), x_proj.T,
        dt_norm_gain.reshape(1, -1), dt_proj, dt_bias.reshape(1, -1), a_log, d_skip.reshape(1, -1),
        query, new_kv, kv_pool, page_sel, lengths.reshape(1, 1),
    )
    hbm = pl.BlockSpec(memory_space=pltpu.HBM)
    vmem = pl.BlockSpec(memory_space=pltpu.VMEM)
    outs = (((16, 256), BF16), ((16, STATE, 256), F32), ((1, 16 * HEAD_DIM), BF16))
    in_smem = {14, 15}
    scratch = [
        (pltpu.SMEM if k in in_smem else pltpu.VMEM)(a.shape, a.dtype) for k, a in enumerate(args)
    ]
    scratch += [
        pltpu.VMEM((16, HEAD_DIM), F32),
        pltpu.VMEM((NZ, 16, HEAD_DIM), BF16),
        pltpu.VMEM((NZ, 1, 128), F32),
        pltpu.VMEM((NZ, 1, 128), F32),
        pltpu.VMEM((NY, 17, 128), F32),
        pltpu.VMEM((NY - 1, 17, 128), F32),
        pltpu.VMEM((16, 128), BF16),
        pltpu.VMEM((1, 128), F32),
        pltpu.VMEM((NZ - 1, 16, 128), BF16),
        pltpu.VMEM((NZ - 1, 1, 128), F32),
        pltpu.VMEM((NY, 17, 128), F32),
        pltpu.VMEM((NZ, 16, HEAD_DIM), BF16),
        pltpu.VMEM((NZ, 1, 128), F32),
        pltpu.VMEM((NZ, 16, HEAD_DIM), BF16),
        pltpu.VMEM((NZ, 1, 128), F32),
        pltpu.VMEM((16, 256), F32),
        pltpu.SemaphoreType.DMA((len(args),)),
    ]
    one, grouped = pltpu.SemaphoreType.DMA, pltpu.SemaphoreType.DMA((len(GROUPS),))
    scratch += [one, grouped, one, grouped, one, one, one, one, one, one, one, one, one, grouped, one, grouped]
    made = pl.pallas_call(
        kernel,
        out_shape=[pltpu.VMEM(*o) for o in outs],
        in_specs=[hbm] * len(args),
        out_specs=[vmem] * 3,
        scratch_shapes=scratch,
        name="decode_step",
        compiler_params=pltpu.CompilerParams(
            collective_id=0, has_side_effects=True, vmem_limit_bytes=60 * 2**20
        ),
    )(*args)
    return pl.pallas_call(
        hand_over,
        out_shape=[jax.ShapeDtypeStruct(*o) for o in outs],
        in_specs=[vmem] * 3,
        out_specs=[hbm] * 3,
        scratch_shapes=[pltpu.SemaphoreType.DMA((3,))],
        name="hand_over",
        compiler_params=pltpu.CompilerParams(vmem_limit_bytes=4 * 2**20),
    )(*made)


def solution(mesh):
    placed = (
        P("req", None, ("head", "ctx")),
        P("req", None, ("head", "ctx")),
        P("req", None, ("head", "ctx")),
        P(None, ("head", "ctx")),
        P(("head", "ctx")),
        P(("head", "ctx"), None),
        P(),
        P(None, ("head", "ctx")),
        P(("head", "ctx")),
        P(None, ("head", "ctx")),
        P(("head", "ctx")),
        P(("req", "ctx"), "head"),
        P(("req", "ctx"), "head"),
        P(("req", "ctx"), None, "head"),
        P(("req", "ctx"), None),
        P(("req", "ctx")),
    )
    return jax.shard_map(
        on_device,
        mesh=mesh,
        in_specs=placed,
        out_specs=(
            P("req", ("head", "ctx")),
            P("req", None, ("head", "ctx")),
            P(("req", "ctx"), "head"),
        ),
        check_vma=False,
    )
```

```python
import functools
import math

import jax
import jax.numpy as jnp
from jax import lax
from jax.experimental import pallas as pl
from jax.experimental.pallas import tpu as pltpu
from jax.sharding import PartitionSpec as P

MESH = pl.DeviceIdType.MESH
STATE = 16
DT_RANK = 512
Q_HEADS = 64
KV_HEADS = 8
HEAD_DIM = 128
PAGE = 64
NZ = 16
NY = 4
POOL = 20
TOPK = 16
EPS = 1e-06
FAR_BELOW = -1e30
FLOOR = -1e29
F32 = jnp.float32
BF16 = jnp.bfloat16

FAR_FIRST = (8, 9, 7, 10, 6, 11, 5, 12, 4, 13, 3, 14, 2, 15, 1)
EARLY = 1
HUB = 4
HUB_ORDER = tuple(t for t in (8, 9, 10, 12, 11, 13, 14, 7, 6, 15, 5, 4, 3, 2, 1) if t >= EARLY and t != HUB)
GROUPS = ((0, EARLY), (EARLY, NZ))
HALF = NZ // 2
SCALE2 = math.log2(math.e) / math.sqrt(HEAD_DIM)
NT = (((1,), (1,)), ((), ()))


def silu(v):
    return v / (1.0 + jnp.exp(-v))


def kernel(
    xz_h, cs_h, ssm_h, cw_h, cb_h, xp_h, gain_h, dtp_h, dtb_h, alog_h, dskip_h,
    q_h, nkv_h, pool_h, sel_h, len_h,
    mamba_v, state_v, attn_v,
    xz_v, cs_v, ssm_v, cw_v, cb_v, xp_v, gain_v, dtp_v, dtb_v, alog_v, dskip_v,
    q_v, nkv_v, pool_v, sel_s, len_s,
    q_own, q_all, sel_all, y_send, y_recv, z_send, zb_send, z_recv, zb_recv, g_recv,
    p_send, pl_send, p_recv, pl_recv, yout,
    load_sem, q_ss, q_rs, c_ss, c_rs, f_ss, fc_ss, y_ss, y_rs, z_ss, z_rs, zb_ss, zb_rs, g_ss, g_rs, p_ss, p_rs, pl_ss, pl_rs,
):
    r = lax.axis_index("req")
    h = lax.axis_index("head")
    c = lax.axis_index("ctx")

    def zpeer(i):
        return (r, h, lax.rem(c + i, NZ))

    def ypeer(i):
        return (r, lax.rem(h + i, NY), c)

    def send(src, dst, ss, rs, dev):
        pltpu.make_async_remote_copy(
            src_ref=src, dst_ref=dst, send_sem=ss, recv_sem=rs, device_id=dev, device_id_type=MESH
        ).start()

    def drain(ref, sem):
        pltpu.make_async_copy(ref, ref, sem).wait()

    is_early = c < EARLY
    is_late = c >= EARLY
    is_hub = c == HUB
    is_rest = is_late & (c != HUB)

    def target_of(i):
        return lax.rem(c + i, NZ)

    barrier = pltpu.get_barrier_semaphore()

    def greet(dev):
        pl.semaphore_signal(barrier, inc=1, device_id=dev, device_id_type=MESH)

    for i in FAR_FIRST:
        pl.when(is_early | is_hub | (target_of(i) >= EARLY))(functools.partial(greet, zpeer(i)))
    for i in range(1, NY):
        greet(ypeer(i))

    pairs = (
        (q_h, q_v), (sel_h, sel_s), (len_h, len_s), (xz_h, xz_v), (cs_h, cs_v), (cw_h, cw_v), (cb_h, cb_v),
        (xp_h, xp_v), (nkv_h, nkv_v), (pool_h, pool_v), (dtp_h, dtp_v), (gain_h, gain_v),
        (dtb_h, dtb_v), (alog_h, alog_v), (dskip_h, dskip_v), (ssm_h, ssm_v),
    )
    loads = [pltpu.make_async_copy(a, b, load_sem.at[k]) for k, (a, b) in enumerate(pairs)]
    for cp in loads:
        cp.start()

    loads[0].wait()
    qrow = q_v[0:1, :].astype(F32)
    for k in range(16):
        q_own[k : k + 1, :] = qrow[:, k * HEAD_DIM : (k + 1) * HEAD_DIM]
    q_all[c] = q_own[...].astype(BF16)

    loads[1].wait()
    loads[2].wait()
    lane = lax.broadcasted_iota(jnp.int32, (1, 128), 1)
    listed = jnp.where(lane == TOPK, len_s[0, 0], -1)
    for k in range(TOPK):
        listed = jnp.where(lane == k, sel_s[0, k], listed)
    sel_all[c] = listed
    z_recv[c] = jnp.zeros((16, 128), BF16)
    zb_recv[c] = jnp.zeros((1, 128), F32)

    @pl.when(is_rest)
    def _():
        z_recv[0:EARLY] = jnp.zeros((EARLY, 16, 128), BF16)
        zb_recv[0:EARLY] = jnp.zeros((EARLY, 1, 128), F32)

    for k in (3, 4, 5, 6):
        loads[k].wait()
    conv = cb_v[0:1, :] + cw_v[3:4, :] * xz_v[:, 0, :].astype(F32)
    for k in range(3):
        conv = conv + cw_v[k : k + 1, :] * cs_v[k].astype(F32)
    mixed_bf = silu(conv).astype(BF16)
    loads[7].wait()
    for j in range(4):
        part = lax.dot_general(mixed_bf, xp_v[j * 128 : (j + 1) * 128, :], NT, preferred_element_type=F32)
        for k in range(NY):
            y_send[k, 4 * j : 4 * j + 4, :] = part[4 * k : 4 * k + 4, :]
    part = lax.dot_general(mixed_bf, xp_v[DT_RANK : DT_RANK + 32, :], NT, preferred_element_type=F32)
    for k in range(NY):
        y_send[k, 16:17, :] = jnp.concatenate([part[4 * k + i : 4 * k + i + 1, :] for i in range(4)], axis=1)

    loads[8].wait()
    nkv = nkv_v[0:1, :].astype(F32)
    half = lax.broadcasted_iota(jnp.int32, (16, HEAD_DIM), 0) < 8
    own_key = jnp.where(half, nkv[:, 0:128], nkv[:, 256:384])
    own_value = jnp.where(half, nkv[:, 128:256], nkv[:, 384:512])
    own_score = jnp.sum(q_own[...] * own_key, axis=1, keepdims=True) * SCALE2
    tokens = POOL * PAGE
    low_half = lane < PAGE
    token = jnp.where(low_half, lane, lane - PAGE)
    entry = jnp.where(lane < POOL, c * POOL + lane, -1)
    for k in range(9, 16):
        loads[k].wait()
    gain = jnp.concatenate(
        [jnp.broadcast_to(gain_v[0:1, j * 128 : (j + 1) * 128], (4, 128)) for j in range(4)], axis=0
    )

    pl.semaphore_wait(barrier, jnp.where(is_early, EARLY, NZ - 1) + NY - 1)

    for i in range(1, NY):
        send(y_send.at[lax.rem(h + i, NY)], y_recv.at[i - 1], y_ss, y_rs, ypeer(i))

    def drain_rows(n, *pairs):
        for ref, sem in pairs:
            drain(ref.at[pl.ds(0, n)], sem)

    def send_query(dev, group):
        send(q_all.at[c], q_all.at[c], q_ss, q_rs.at[group], dev)
        send(sel_all.at[c], sel_all.at[c], c_ss, c_rs.at[group], dev)

    @pl.when(is_early)
    def _():
        for to in (HUB, *range(EARLY)):
            pl.when(c != to)(functools.partial(send_query, (r, h, jnp.int32(to)), 0))

    @pl.when(is_hub)
    def _():
        drain_rows(EARLY, (q_all, q_rs.at[0]), (sel_all, c_rs.at[0]))
        block = pl.ds(0, EARLY)
        for k, to in enumerate(HUB_ORDER):
            dev = (r, h, jnp.int32(to))
            send(q_all.at[block], q_all.at[block], f_ss.at[k], q_rs.at[0], dev)
            send(sel_all.at[block], sel_all.at[block], fc_ss.at[k], c_rs.at[0], dev)

    @pl.when(is_late)
    def _():
        for i in FAR_FIRST:
            send_query(zpeer(i), 1)

    total = y_send[h]
    drain(y_recv, y_rs)
    for i in range(NY - 1):
        total = total + y_recv[i]
    z_send[0] = total[0:16].astype(BF16)
    zb_send[0] = total[16:17]

    def send_sums(dev, which, group):
        send(z_send.at[which], z_recv.at[c], z_ss, z_rs.at[group], dev)
        send(zb_send.at[which], zb_recv.at[c], zb_ss, zb_rs.at[group], dev)

    @pl.when(is_early)
    def _():
        for to in (HUB, *range(EARLY)):
            pl.when(c != to)(functools.partial(send_sums, (r, h, jnp.int32(to)), 0, 0))

    @pl.when(is_hub)
    def _():
        drain_rows(EARLY, (z_recv, z_rs.at[0]), (zb_recv, zb_rs.at[0]))
        z_send[1] = (total[0:16] + jnp.sum(z_recv[0:EARLY].astype(F32), axis=0)).astype(BF16)
        zb_send[1] = total[16:17] + jnp.sum(zb_recv[0:EARLY], axis=0)
        for to in range(EARLY):
            send_sums((r, h, jnp.int32(to)), 0, 1)
        for to in HUB_ORDER:
            send_sums((r, h, jnp.int32(to)), 1, 1)

    @pl.when(is_rest)
    def _():
        for to in range(EARLY):
            send_sums((r, h, jnp.int32(to)), 0, 1)
        for i in FAR_FIRST:
            pl.when(target_of(i) >= EARLY)(functools.partial(send_sums, zpeer(i), 0, 1))

    diagonal = (
        lax.broadcasted_iota(jnp.int32, (1, 16, HEAD_DIM), 1)
        == lax.broadcasted_iota(jnp.int32, (1, 16, HEAD_DIM), 2)
    )
    for g, (first, last) in enumerate(GROUPS):
        n = last - first
        arrivals = (q_all, q_rs.at[g]), (sel_all, c_rs.at[g])
        if g == 0:
            pl.when(is_early)(functools.partial(drain_rows, EARLY - 1, *arrivals))
            pl.when(is_rest)(functools.partial(drain_rows, EARLY, *arrivals))
        else:
            pl.when(is_early)(functools.partial(drain_rows, NZ - EARLY, *arrivals))
            pl.when(is_late)(functools.partial(drain_rows, NZ - EARLY - 1, *arrivals))
        listed = sel_all[first:last, 0, :]
        counts = jnp.zeros((n, 128), jnp.int32)
        for k in range(TOPK):
            amount = listed[:, TOPK : TOPK + 1] if k == 0 else PAGE
            counts = jnp.where(listed[:, k : k + 1] == entry, amount, counts)
        bias = jnp.concatenate(
            [
                jnp.where(
                    token < jnp.where(low_half, counts[:, 2 * j : 2 * j + 1], counts[:, 2 * j + 1 : 2 * j + 2]),
                    0.0,
                    FAR_BELOW,
                )
                for j in range(POOL // 2)
            ],
            axis=1,
        )
        queries = q_all[first:last].astype(F32)
        outs, levels = [], []
        for v in range(2):
            qv = queries[:, 8 * v : 8 * v + 8, :].reshape(n * 8, HEAD_DIM).astype(BF16)
            keys = pool_v[:, :, 256 * v : 256 * v + 128].reshape(tokens, HEAD_DIM)
            values = pool_v[:, :, 256 * v + 128 : 256 * v + 256].reshape(tokens, HEAD_DIM)
            s = lax.dot_general(qv, keys, NT, preferred_element_type=F32) * SCALE2
            s = s.reshape(n, 8, tokens) + bias[:, None, :]
            top = jnp.maximum(jnp.max(s, axis=2, keepdims=True), FLOOR)
            w = jnp.exp2(s - top).astype(BF16)
            weight_sum = jnp.sum(w.astype(F32), axis=2, keepdims=True)
            o = jnp.dot(w.reshape(n * 8, tokens), values, preferred_element_type=F32).reshape(n, 8, HEAD_DIM)
            kept = jnp.maximum(weight_sum, 1.0)
            outs.append(o / kept)
            levels.append(top + jnp.log2(kept))
        level = jnp.concatenate(levels, axis=1)
        p_send[first:last] = jnp.concatenate(outs, axis=1).astype(BF16)
        pl_send[first:last] = jnp.sum(jnp.where(diagonal, level, 0.0), axis=1, keepdims=True)

        def send_part(to):
            dev = (r, h, jnp.int32(to))
            send(p_send.at[to], p_recv.at[c], p_ss, p_rs.at[c // HALF], dev)
            send(pl_send.at[to], pl_recv.at[c], pl_ss, pl_rs.at[c // HALF], dev)

        for to in range(first, last):
            pl.when(c != to)(functools.partial(send_part, to))

    total = total[0:16]
    terms = zb_send[0]
    pl.when(is_early)(functools.partial(drain_rows, EARLY - 1, (z_recv, z_rs.at[0]), (zb_recv, zb_rs.at[0])))
    others = (z_recv, z_rs.at[1]), (zb_recv, zb_rs.at[1])
    pl.when(is_early)(functools.partial(drain_rows, NZ - EARLY, *others))
    pl.when(is_late)(functools.partial(drain_rows, NZ - EARLY - 1, *others))
    total = total + jnp.sum(z_recv[...].astype(F32), axis=0)
    terms = terms + jnp.sum(zb_recv[...], axis=0)
    square = total * total
    square = square[0:8] + square[8:16]
    square = square + jnp.concatenate([square[4:8], square[0:4]], axis=0)
    square = jnp.sum(square, axis=1, keepdims=True) * (1.0 / DT_RANK)
    inv = lax.rsqrt(square + EPS)
    g_recv[h, 0:16, :] = total * jnp.concatenate([inv, inv], axis=0) * gain
    g_recv[h, 16:17, :] = terms
    for i in range(1, NY):
        send(g_recv.at[h], g_recv.at[h], g_ss, g_rs, ypeer(i))
    rate = jnp.exp(alog_v[...])
    gate = silu(xz_v[:, 1, :].astype(F32))
    mixed = mixed_bf.astype(F32)
    drain(y_recv, g_rs)

    step = dtb_v[0:1, :]
    for j in range(4):
        normed = jnp.concatenate([g_recv[k, 4 * j : 4 * j + 4, :] for k in range(NY)], axis=0).astype(BF16)
        step = step + jnp.dot(normed, dtp_v[j * 128 : (j + 1) * 128, :], preferred_element_type=F32)
    step = jnp.maximum(step, 0.0) + jnp.log1p(jnp.exp(-jnp.abs(step)))
    terms = jnp.concatenate([g_recv[k, 16:17, :] for k in range(NY)] + [jnp.zeros((124, 128), F32)], axis=0).T
    drive = step * mixed
    for i in range(16):
        k, low = i // 4, 32 * (i % 4)
        decay = jnp.exp(-(step[i : i + 1, :] * rate))
        new = decay * ssm_v[i] + drive[i : i + 1, :] * terms[low : low + 16, k : k + 1]
        state_v[i] = new
        yout[i : i + 1, :] = jnp.sum(terms[low + 16 : low + 32, k : k + 1] * new, axis=0, keepdims=True)
    mamba_v[...] = ((yout[...] + dskip_v[0:1, :] * mixed) * gate).astype(BF16)

    p_recv[c] = p_send[c]
    pl_recv[c] = pl_send[c]
    top, weight, summed = own_score, jnp.ones_like(own_score), own_value
    for g, (first, last) in enumerate(((0, HALF), (HALF, NZ))):
        arrivals = (pl_recv, pl_rs.at[g]), (p_recv, p_rs.at[g])
        pl.when(c // HALF == g)(functools.partial(drain_rows, HALF - 1, *arrivals))
        pl.when(c // HALF != g)(functools.partial(drain_rows, HALF, *arrivals))
        level = jnp.sum(jnp.where(diagonal, pl_recv[first:last], 0.0), axis=2, keepdims=True)
        new_top = jnp.maximum(top, jnp.max(level, axis=0))
        old = jnp.exp2(top - new_top)
        w = jnp.exp2(level - new_top[None])
        weight = weight * old + jnp.sum(w, axis=0)
        summed = summed * old + jnp.sum(w * p_recv[first:last].astype(F32), axis=0)
        top = new_top
    joined = (summed / weight).astype(BF16)
    for k in range(16):
        attn_v[0:1, k * HEAD_DIM : (k + 1) * HEAD_DIM] = joined[k : k + 1, :]

    drain(y_recv, y_ss)
    drain(y_recv, g_ss)
    drain_rows(NZ - 1, (p_recv, p_ss), (pl_recv, pl_ss))
    sent = (q_all, q_ss), (sel_all, c_ss), (z_recv, z_ss), (zb_recv, zb_ss)
    pl.when(is_early)(functools.partial(drain_rows, EARLY, *sent))
    pl.when(is_late)(functools.partial(drain_rows, NZ - 1, *sent))

    @pl.when(is_hub)
    def _():
        for k in range(len(HUB_ORDER)):
            drain_rows(EARLY, (q_all, f_ss.at[k]), (sel_all, fc_ss.at[k]))


def hand_over(a_in, b_in, c_in, a_out, b_out, c_out, sem):
    copies = [
        pltpu.make_async_copy(x, y, sem.at[k])
        for k, (x, y) in enumerate(((a_in, a_out), (b_in, b_out), (c_in, c_out)))
    ]
    for cp in copies:
        cp.start()
    for cp in copies:
        cp.wait()


def on_device(
    xz, conv_state, ssm_state, conv_weight, conv_bias, x_proj, dt_norm_gain, dt_proj, dt_bias, a_log, d_skip,
    query, new_kv, kv_pool, page_sel, lengths,
):
    args = (
        xz, conv_state.transpose(1, 0, 2), ssm_state, conv_weight, conv_bias.reshape(1, -1), x_proj.T,
        dt_norm_gain.reshape(1, -1), dt_proj, dt_bias.reshape(1, -1), a_log, d_skip.reshape(1, -1),
        query, new_kv, kv_pool, page_sel, lengths.reshape(1, 1),
    )
    hbm = pl.BlockSpec(memory_space=pltpu.HBM)
    vmem = pl.BlockSpec(memory_space=pltpu.VMEM)
    outs = (((16, 256), BF16), ((16, STATE, 256), F32), ((1, 16 * HEAD_DIM), BF16))
    in_smem = {14, 15}
    scratch = [
        (pltpu.SMEM if k in in_smem else pltpu.VMEM)(a.shape, a.dtype) for k, a in enumerate(args)
    ]
    scratch += [
        pltpu.VMEM((16, HEAD_DIM), F32),
        pltpu.VMEM((NZ, 16, HEAD_DIM), BF16),
        pltpu.VMEM((NZ, 1, 128), jnp.int32),
        pltpu.VMEM((NY, 17, 128), F32),
        pltpu.VMEM((NY - 1, 17, 128), F32),
        pltpu.VMEM((2, 16, 128), BF16),
        pltpu.VMEM((2, 1, 128), F32),
        pltpu.VMEM((NZ, 16, 128), BF16),
        pltpu.VMEM((NZ, 1, 128), F32),
        pltpu.VMEM((NY, 17, 128), F32),
        pltpu.VMEM((NZ, 16, HEAD_DIM), BF16),
        pltpu.VMEM((NZ, 1, 128), F32),
        pltpu.VMEM((NZ, 16, HEAD_DIM), BF16),
        pltpu.VMEM((NZ, 1, 128), F32),
        pltpu.VMEM((16, 256), F32),
        pltpu.SemaphoreType.DMA((len(args),)),
    ]
    one, two = pltpu.SemaphoreType.DMA, pltpu.SemaphoreType.DMA((2,))
    scratch += [one, two, one, two] + [pltpu.SemaphoreType.DMA((len(HUB_ORDER),))] * 2
    scratch += [one, one, one, two, one, two, one, one, one, two, one, two]
    made = pl.pallas_call(
        kernel,
        out_shape=[pltpu.VMEM(*o) for o in outs],
        in_specs=[hbm] * len(args),
        out_specs=[vmem] * 3,
        scratch_shapes=scratch,
        name="decode_step",
        compiler_params=pltpu.CompilerParams(
            collective_id=0, has_side_effects=True, vmem_limit_bytes=60 * 2**20
        ),
    )(*args)
    return pl.pallas_call(
        hand_over,
        out_shape=[jax.ShapeDtypeStruct(*o) for o in outs],
        in_specs=[vmem] * 3,
        out_specs=[hbm] * 3,
        scratch_shapes=[pltpu.SemaphoreType.DMA((3,))],
        name="hand_over",
        compiler_params=pltpu.CompilerParams(vmem_limit_bytes=4 * 2**20),
    )(*made)


def solution(mesh):
    placed = (
        P("req", None, ("head", "ctx")),
        P("req", None, ("head", "ctx")),
        P("req", None, ("head", "ctx")),
        P(None, ("head", "ctx")),
        P(("head", "ctx")),
        P(("head", "ctx"), None),
        P(),
        P(None, ("head", "ctx")),
        P(("head", "ctx")),
        P(None, ("head", "ctx")),
        P(("head", "ctx")),
        P(("req", "ctx"), "head"),
        P(("req", "ctx"), "head"),
        P(("req", "ctx"), None, "head"),
        P(("req", "ctx"), None),
        P(("req", "ctx")),
    )
    return jax.shard_map(
        on_device,
        mesh=mesh,
        in_specs=placed,
        out_specs=(
            P("req", ("head", "ctx")),
            P("req", None, ("head", "ctx")),
            P(("req", "ctx"), "head"),
        ),
        check_vma=False,
    )
```

```python
import functools
import math

import jax
import jax.numpy as jnp
from jax import lax
from jax.experimental import pallas as pl
from jax.experimental.pallas import tpu as pltpu
from jax.sharding import PartitionSpec as P

MESH = pl.DeviceIdType.MESH
STATE = 16
DT_RANK = 512
Q_HEADS = 64
KV_HEADS = 8
HEAD_DIM = 128
PAGE = 64
NZ = 16
NY = 4
POOL = 20
TOPK = 16
EPS = 1e-06
FAR_BELOW = -1e30
FLOOR = -1e29
F32 = jnp.float32
BF16 = jnp.bfloat16

FAR_FIRST = (8, 9, 7, 10, 6, 11, 5, 12, 4, 13, 3, 14, 2, 15, 1)
EARLY = 1
APART = 4
FORWARD_ORDER = (8, 9, 10, 12, 11, 13, 14, 7, 6, 15, 5, 4, 3, 2, 1)
GROUPS = ((0, EARLY), (EARLY, NZ // 2), (NZ // 2, NZ))
HALF = NZ // 2
SCALE2 = math.log2(math.e) / math.sqrt(HEAD_DIM)
NT = (((1,), (1,)), ((), ()))


def silu(v):
    return v / (1.0 + jnp.exp(-v))


def kernel(
    xz_h, cs_h, ssm_h, cw_h, cb_h, xp_h, gain_h, dtp_h, dtb_h, alog_h, dskip_h,
    q_h, nkv_h, pool_h, sel_h, len_h,
    mamba_v, state_v, attn_v,
    xz_v, cs_v, ssm_v, cw_v, cb_v, xp_v, gain_v, dtp_v, dtb_v, alog_v, dskip_v,
    q_v, nkv_v, pool_v, sel_s, len_s,
    q_own, q_all, sel_all, y_send, y_recv, z_send, zb_send, z_recv, zb_recv, g_recv,
    p_send, pl_send, p_recv, pl_recv, yout,
    load_sem, q_ss, q_rs, c_ss, c_rs, f_ss, fc_ss, y_ss, y_rs, z_ss, z_rs, zb_ss, zb_rs, g_ss, g_rs, p_ss, p_rs, pl_ss, pl_rs,
):
    r = lax.axis_index("req")
    h = lax.axis_index("head")
    c = lax.axis_index("ctx")

    def zpeer(i):
        return (r, h, lax.rem(c + i, NZ))

    def ypeer(i):
        return (r, lax.rem(h + i, NY), c)

    def send(src, dst, ss, rs, dev):
        pltpu.make_async_remote_copy(
            src_ref=src, dst_ref=dst, send_sem=ss, recv_sem=rs, device_id=dev, device_id_type=MESH
        ).start()

    def drain(ref, sem):
        pltpu.make_async_copy(ref, ref, sem).wait()

    is_early = c < EARLY
    is_late = c >= EARLY
    mine = c - APART
    is_hub = (mine >= 0) & (mine < EARLY)
    is_rest = is_late & jnp.logical_not(is_hub)

    def target_of(i):
        return lax.rem(c + i, NZ)

    barrier = pltpu.get_barrier_semaphore()

    def greet(dev):
        pl.semaphore_signal(barrier, inc=1, device_id=dev, device_id_type=MESH)

    for i in FAR_FIRST:
        pl.when(is_early | (target_of(i) >= EARLY) | (is_hub & (target_of(i) == mine)))(functools.partial(greet, zpeer(i)))
    for i in range(1, NY):
        greet(ypeer(i))

    pairs = (
        (q_h, q_v), (sel_h, sel_s), (len_h, len_s), (xz_h, xz_v), (cs_h, cs_v), (cw_h, cw_v), (cb_h, cb_v),
        (xp_h, xp_v), (nkv_h, nkv_v), (pool_h, pool_v), (dtp_h, dtp_v), (gain_h, gain_v),
        (dtb_h, dtb_v), (alog_h, alog_v), (dskip_h, dskip_v), (ssm_h, ssm_v),
    )
    loads = [pltpu.make_async_copy(a, b, load_sem.at[k]) for k, (a, b) in enumerate(pairs)]
    for cp in loads:
        cp.start()

    loads[0].wait()
    qrow = q_v[0:1, :].astype(F32)
    for k in range(16):
        q_own[k : k + 1, :] = qrow[:, k * HEAD_DIM : (k + 1) * HEAD_DIM]
    q_all[c] = q_own[...].astype(BF16)

    loads[1].wait()
    loads[2].wait()
    lane = lax.broadcasted_iota(jnp.int32, (1, 128), 1)
    listed = jnp.where(lane == TOPK, len_s[0, 0], -1)
    for k in range(TOPK):
        listed = jnp.where(lane == k, sel_s[0, k], listed)
    sel_all[c] = listed
    z_recv[c] = jnp.zeros((16, 128), BF16)
    zb_recv[c] = jnp.zeros((1, 128), F32)

    for e in range(EARLY):

        @pl.when(is_late & (mine != e))
        def _():
            z_recv[e] = jnp.zeros((16, 128), BF16)
            zb_recv[e] = jnp.zeros((1, 128), F32)

    for k in (3, 4, 5, 6):
        loads[k].wait()
    conv = cb_v[0:1, :] + cw_v[3:4, :] * xz_v[:, 0, :].astype(F32)
    for k in range(3):
        conv = conv + cw_v[k : k + 1, :] * cs_v[k].astype(F32)
    mixed_bf = silu(conv).astype(BF16)
    loads[7].wait()
    for j in range(4):
        part = lax.dot_general(mixed_bf, xp_v[j * 128 : (j + 1) * 128, :], NT, preferred_element_type=F32)
        for k in range(NY):
            y_send[k, 4 * j : 4 * j + 4, :] = part[4 * k : 4 * k + 4, :]
    part = lax.dot_general(mixed_bf, xp_v[DT_RANK : DT_RANK + 32, :], NT, preferred_element_type=F32)
    for k in range(NY):
        y_send[k, 16:17, :] = jnp.concatenate([part[4 * k + i : 4 * k + i + 1, :] for i in range(4)], axis=1)

    loads[8].wait()
    nkv = nkv_v[0:1, :].astype(F32)
    half = lax.broadcasted_iota(jnp.int32, (16, HEAD_DIM), 0) < 8
    own_key = jnp.where(half, nkv[:, 0:128], nkv[:, 256:384])
    own_value = jnp.where(half, nkv[:, 128:256], nkv[:, 384:512])
    own_score = jnp.sum(q_own[...] * own_key, axis=1, keepdims=True) * SCALE2
    tokens = POOL * PAGE
    low_half = lane < PAGE
    token = jnp.where(low_half, lane, lane - PAGE)
    entry = jnp.where(lane < POOL, c * POOL + lane, -1)
    for k in range(9, 16):
        loads[k].wait()
    gain = jnp.concatenate(
        [jnp.broadcast_to(gain_v[0:1, j * 128 : (j + 1) * 128], (4, 128)) for j in range(4)], axis=0
    )

    pl.semaphore_wait(barrier, jnp.where(is_early, EARLY, NZ - 1) + NY - 1)

    for i in range(1, NY):
        send(y_send.at[lax.rem(h + i, NY)], y_recv.at[i - 1], y_ss, y_rs, ypeer(i))

    def drain_rows(n, *pairs):
        for ref, sem in pairs:
            drain(ref.at[pl.ds(0, n)], sem)

    def send_query(dev, group):
        send(q_all.at[c], q_all.at[c], q_ss, q_rs.at[group], dev)
        send(sel_all.at[c], sel_all.at[c], c_ss, c_rs.at[group], dev)

    def each_early(act):
        for to in range(EARLY):
            pl.when(c != to)(functools.partial(act, (r, h, jnp.int32(to))))

    def each_late(act):
        for to in FORWARD_ORDER:
            if to >= EARLY:
                pl.when(c != to)(functools.partial(act, (r, h, jnp.int32(to))))

    @pl.when(is_early)
    def _():
        send_query((r, h, c + APART), 3)
        each_early(lambda dev: send_query(dev, 0))

    @pl.when(is_hub)
    def _():
        drain_rows(1, (q_all, q_rs.at[3]), (sel_all, c_rs.at[3]))

        def forward(dev):
            send(q_all.at[mine], q_all.at[mine], f_ss, q_rs.at[0], dev)
            send(sel_all.at[mine], sel_all.at[mine], fc_ss, c_rs.at[0], dev)

        each_late(forward)

    @pl.when(is_late)
    def _():
        for i in FAR_FIRST:
            send_query(zpeer(i), 1 + c // HALF)

    total = y_send[h]
    drain(y_recv, y_rs)
    for i in range(NY - 1):
        total = total + y_recv[i]
    z_send[0] = total[0:16].astype(BF16)
    zb_send[0] = total[16:17]

    def send_sums(dev, which, group):
        send(z_send.at[which], z_recv.at[c], z_ss, z_rs.at[group], dev)
        send(zb_send.at[which], zb_recv.at[c], zb_ss, zb_rs.at[group], dev)

    @pl.when(is_early)
    def _():
        send_sums((r, h, c + APART), 0, 2)
        each_early(lambda dev: send_sums(dev, 0, 0))

    @pl.when(is_hub)
    def _():
        drain_rows(1, (z_recv, z_rs.at[2]), (zb_recv, zb_rs.at[2]))
        z_send[1] = (total[0:16] + z_recv[mine].astype(F32)).astype(BF16)
        zb_send[1] = total[16:17] + zb_recv[mine]
        each_early(lambda dev: send_sums(dev, 0, 1))
        each_late(lambda dev: send_sums(dev, 1, 1))

    @pl.when(is_rest)
    def _():
        for to in range(EARLY):
            send_sums((r, h, jnp.int32(to)), 0, 1)
        for i in FAR_FIRST:
            pl.when(target_of(i) >= EARLY)(functools.partial(send_sums, zpeer(i), 0, 1))

    own_total = total

    def finish_sums():
        total = own_total[0:16]
        terms = zb_send[0]
        if EARLY > 1:
            pl.when(is_early)(functools.partial(drain_rows, EARLY - 1, (z_recv, z_rs.at[0]), (zb_recv, zb_rs.at[0])))
        others = (z_recv, z_rs.at[1]), (zb_recv, zb_rs.at[1])
        pl.when(is_early)(functools.partial(drain_rows, NZ - EARLY, *others))
        pl.when(is_late)(functools.partial(drain_rows, NZ - EARLY - 1, *others))
        total = total + jnp.sum(z_recv[...].astype(F32), axis=0)
        terms = terms + jnp.sum(zb_recv[...], axis=0)
        square = total * total
        square = square[0:8] + square[8:16]
        square = square + jnp.concatenate([square[4:8], square[0:4]], axis=0)
        square = jnp.sum(square, axis=1, keepdims=True) * (1.0 / DT_RANK)
        inv = lax.rsqrt(square + EPS)
        g_recv[h, 0:16, :] = total * jnp.concatenate([inv, inv], axis=0) * gain
        g_recv[h, 16:17, :] = terms
        for i in range(1, NY):
            send(g_recv.at[h], g_recv.at[h], g_ss, g_rs, ypeer(i))

    diagonal = (
        lax.broadcasted_iota(jnp.int32, (1, 16, HEAD_DIM), 1)
        == lax.broadcasted_iota(jnp.int32, (1, 16, HEAD_DIM), 2)
    )
    for g, (first, last) in enumerate(GROUPS):
        n = last - first
        arrivals = (q_all, q_rs.at[g]), (sel_all, c_rs.at[g])
        if g == 0:
            pl.when(is_rest)(functools.partial(drain_rows, EARLY, *arrivals))
            if EARLY > 1:
                pl.when(is_early | is_hub)(functools.partial(drain_rows, EARLY - 1, *arrivals))
        else:
            if g == 2:
                pl.when(is_early)(finish_sums)
            inside = (c >= first) & (c < last)
            pl.when(inside)(functools.partial(drain_rows, n - 1, *arrivals))
            pl.when(jnp.logical_not(inside))(functools.partial(drain_rows, n, *arrivals))
        listed = sel_all[first:last, 0, :]
        counts = jnp.zeros((n, 128), jnp.int32)
        for k in range(TOPK):
            amount = listed[:, TOPK : TOPK + 1] if k == 0 else PAGE
            counts = jnp.where(listed[:, k : k + 1] == entry, amount, counts)
        bias = jnp.concatenate(
            [
                jnp.where(
                    token < jnp.where(low_half, counts[:, 2 * j : 2 * j + 1], counts[:, 2 * j + 1 : 2 * j + 2]),
                    0.0,
                    FAR_BELOW,
                )
                for j in range(POOL // 2)
            ],
            axis=1,
        )
        queries = q_all[first:last].astype(F32)
        outs, levels = [], []
        for v in range(2):
            qv = queries[:, 8 * v : 8 * v + 8, :].reshape(n * 8, HEAD_DIM).astype(BF16)
            keys = pool_v[:, :, 256 * v : 256 * v + 128].reshape(tokens, HEAD_DIM)
            values = pool_v[:, :, 256 * v + 128 : 256 * v + 256].reshape(tokens, HEAD_DIM)
            s = lax.dot_general(qv, keys, NT, preferred_element_type=F32) * SCALE2
            s = s.reshape(n, 8, tokens) + bias[:, None, :]
            top = jnp.maximum(jnp.max(s, axis=2, keepdims=True), FLOOR)
            w = jnp.exp2(s - top).astype(BF16)
            weight_sum = jnp.sum(w.astype(F32), axis=2, keepdims=True)
            o = jnp.dot(w.reshape(n * 8, tokens), values, preferred_element_type=F32).reshape(n, 8, HEAD_DIM)
            kept = jnp.maximum(weight_sum, 1.0)
            outs.append(o / kept)
            levels.append(top + jnp.log2(kept))
        level = jnp.concatenate(levels, axis=1)
        p_send[first:last] = jnp.concatenate(outs, axis=1).astype(BF16)
        pl_send[first:last] = jnp.sum(jnp.where(diagonal, level, 0.0), axis=1, keepdims=True)

        def send_part(to):
            dev = (r, h, jnp.int32(to))
            send(p_send.at[to], p_recv.at[c], p_ss, p_rs.at[c // HALF], dev)
            send(pl_send.at[to], pl_recv.at[c], pl_ss, pl_rs.at[c // HALF], dev)

        for to in range(first, last):
            pl.when(c != to)(functools.partial(send_part, to))

    pl.when(is_late)(finish_sums)
    rate = jnp.exp(alog_v[...])
    gate = silu(xz_v[:, 1, :].astype(F32))
    mixed = mixed_bf.astype(F32)
    drain(y_recv, g_rs)

    step = dtb_v[0:1, :]
    for j in range(4):
        normed = jnp.concatenate([g_recv[k, 4 * j : 4 * j + 4, :] for k in range(NY)], axis=0).astype(BF16)
        step = step + jnp.dot(normed, dtp_v[j * 128 : (j + 1) * 128, :], preferred_element_type=F32)
    step = jnp.maximum(step, 0.0) + jnp.log1p(jnp.exp(-jnp.abs(step)))
    terms = jnp.concatenate([g_recv[k, 16:17, :] for k in range(NY)] + [jnp.zeros((124, 128), F32)], axis=0).T
    drive = step * mixed
    for i in range(16):
        k, low = i // 4, 32 * (i % 4)
        decay = jnp.exp(-(step[i : i + 1, :] * rate))
        new = decay * ssm_v[i] + drive[i : i + 1, :] * terms[low : low + 16, k : k + 1]
        state_v[i] = new
        yout[i : i + 1, :] = jnp.sum(terms[low + 16 : low + 32, k : k + 1] * new, axis=0, keepdims=True)
    mamba_v[...] = ((yout[...] + dskip_v[0:1, :] * mixed) * gate).astype(BF16)

    p_recv[c] = p_send[c]
    pl_recv[c] = pl_send[c]
    top, weight, summed = own_score, jnp.ones_like(own_score), own_value
    for g, (first, last) in enumerate(((0, HALF), (HALF, NZ))):
        arrivals = (pl_recv, pl_rs.at[g]), (p_recv, p_rs.at[g])
        pl.when(c // HALF == g)(functools.partial(drain_rows, HALF - 1, *arrivals))
        pl.when(c // HALF != g)(functools.partial(drain_rows, HALF, *arrivals))
        level = jnp.sum(jnp.where(diagonal, pl_recv[first:last], 0.0), axis=2, keepdims=True)
        new_top = jnp.maximum(top, jnp.max(level, axis=0))
        old = jnp.exp2(top - new_top)
        w = jnp.exp2(level - new_top[None])
        weight = weight * old + jnp.sum(w, axis=0)
        summed = summed * old + jnp.sum(w * p_recv[first:last].astype(F32), axis=0)
        top = new_top
    joined = (summed / weight).astype(BF16)
    for k in range(16):
        attn_v[0:1, k * HEAD_DIM : (k + 1) * HEAD_DIM] = joined[k : k + 1, :]

    drain(y_recv, y_ss)
    drain(y_recv, g_ss)
    drain_rows(NZ - 1, (p_recv, p_ss), (pl_recv, pl_ss))
    sent = (q_all, q_ss), (sel_all, c_ss), (z_recv, z_ss), (zb_recv, zb_ss)
    pl.when(is_early)(functools.partial(drain_rows, EARLY, *sent))
    pl.when(is_late)(functools.partial(drain_rows, NZ - 1, *sent))

    pl.when(is_hub)(functools.partial(drain_rows, NZ - EARLY - 1, (q_all, f_ss), (sel_all, fc_ss)))


def hand_over(a_in, b_in, c_in, a_out, b_out, c_out, sem):
    copies = [
        pltpu.make_async_copy(x, y, sem.at[k])
        for k, (x, y) in enumerate(((a_in, a_out), (b_in, b_out), (c_in, c_out)))
    ]
    for cp in copies:
        cp.start()
    for cp in copies:
        cp.wait()


def on_device(
    xz, conv_state, ssm_state, conv_weight, conv_bias, x_proj, dt_norm_gain, dt_proj, dt_bias, a_log, d_skip,
    query, new_kv, kv_pool, page_sel, lengths,
):
    args = (
        xz, conv_state.transpose(1, 0, 2), ssm_state, conv_weight, conv_bias.reshape(1, -1), x_proj.T,
        dt_norm_gain.reshape(1, -1), dt_proj, dt_bias.reshape(1, -1), a_log, d_skip.reshape(1, -1),
        query, new_kv, kv_pool, page_sel, lengths.reshape(1, 1),
    )
    hbm = pl.BlockSpec(memory_space=pltpu.HBM)
    vmem = pl.BlockSpec(memory_space=pltpu.VMEM)
    outs = (((16, 256), BF16), ((16, STATE, 256), F32), ((1, 16 * HEAD_DIM), BF16))
    in_smem = {14, 15}
    scratch = [
        (pltpu.SMEM if k in in_smem else pltpu.VMEM)(a.shape, a.dtype) for k, a in enumerate(args)
    ]
    scratch += [
        pltpu.VMEM((16, HEAD_DIM), F32),
        pltpu.VMEM((NZ, 16, HEAD_DIM), BF16),
        pltpu.VMEM((NZ, 1, 128), jnp.int32),
        pltpu.VMEM((NY, 17, 128), F32),
        pltpu.VMEM((NY - 1, 17, 128), F32),
        pltpu.VMEM((2, 16, 128), BF16),
        pltpu.VMEM((2, 1, 128), F32),
        pltpu.VMEM((NZ, 16, 128), BF16),
        pltpu.VMEM((NZ, 1, 128), F32),
        pltpu.VMEM((NY, 17, 128), F32),
        pltpu.VMEM((NZ, 16, HEAD_DIM), BF16),
        pltpu.VMEM((NZ, 1, 128), F32),
        pltpu.VMEM((NZ, 16, HEAD_DIM), BF16),
        pltpu.VMEM((NZ, 1, 128), F32),
        pltpu.VMEM((16, 256), F32),
        pltpu.SemaphoreType.DMA((len(args),)),
    ]
    one, two = pltpu.SemaphoreType.DMA, pltpu.SemaphoreType.DMA((2,))
    three = pltpu.SemaphoreType.DMA((3,))
    four = pltpu.SemaphoreType.DMA((4,))
    scratch += [one, four, one, four, one, one, one, one, one, three, one, three, one, one, one, two, one, two]
    made = pl.pallas_call(
        kernel,
        out_shape=[pltpu.VMEM(*o) for o in outs],
        in_specs=[hbm] * len(args),
        out_specs=[vmem] * 3,
        scratch_shapes=scratch,
        name="decode_step",
        compiler_params=pltpu.CompilerParams(
            collective_id=0, has_side_effects=True, vmem_limit_bytes=60 * 2**20
        ),
    )(*args)
    return pl.pallas_call(
        hand_over,
        out_shape=[jax.ShapeDtypeStruct(*o) for o in outs],
        in_specs=[vmem] * 3,
        out_specs=[hbm] * 3,
        scratch_shapes=[pltpu.SemaphoreType.DMA((3,))],
        name="hand_over",
        compiler_params=pltpu.CompilerParams(vmem_limit_bytes=4 * 2**20),
    )(*made)


def solution(mesh):
    placed = (
        P("req", None, ("head", "ctx")),
        P("req", None, ("head", "ctx")),
        P("req", None, ("head", "ctx")),
        P(None, ("head", "ctx")),
        P(("head", "ctx")),
        P(("head", "ctx"), None),
        P(),
        P(None, ("head", "ctx")),
        P(("head", "ctx")),
        P(None, ("head", "ctx")),
        P(("head", "ctx")),
        P(("req", "ctx"), "head"),
        P(("req", "ctx"), "head"),
        P(("req", "ctx"), None, "head"),
        P(("req", "ctx"), None),
        P(("req", "ctx")),
    )
    return jax.shard_map(
        on_device,
        mesh=mesh,
        in_specs=placed,
        out_specs=(
            P("req", ("head", "ctx")),
            P("req", None, ("head", "ctx")),
            P(("req", "ctx"), "head"),
        ),
        check_vma=False,
    )
```

```python
import functools
import math

import jax
import jax.numpy as jnp
from jax import lax
from jax.experimental import pallas as pl
from jax.experimental.pallas import tpu as pltpu
from jax.sharding import PartitionSpec as P

MESH = pl.DeviceIdType.MESH
STATE = 16
DT_RANK = 512
Q_HEADS = 64
KV_HEADS = 8
HEAD_DIM = 128
PAGE = 64
NZ = 16
NY = 4
POOL = 20
TOPK = 16
EPS = 1e-06
FAR_BELOW = -1e30
FLOOR = -1e29
F32 = jnp.float32
BF16 = jnp.bfloat16

FAR_FIRST = (8, 9, 7, 10, 6, 11, 5, 12, 4, 13, 3, 14, 2, 15, 1)
EARLY = 1
APART = 4
FORWARD_ORDER = (8, 9, 10, 12, 11, 13, 14, 7, 6, 15, 5, 4, 3, 2, 1)
GROUPS = ((0, EARLY), (EARLY, 4), (4, NZ // 2), (NZ // 2, NZ))
HALF = NZ // 2
SCALE2 = math.log2(math.e) / math.sqrt(HEAD_DIM)
NT = (((1,), (1,)), ((), ()))


def silu(v):
    return v / (1.0 + jnp.exp(-v))


def kernel(
    xz_h, cs_h, ssm_h, cw_h, cb_h, xp_h, gain_h, dtp_h, dtb_h, alog_h, dskip_h,
    q_h, nkv_h, pool_h, sel_h, len_h,
    mamba_v, state_v, attn_v,
    xz_v, cs_v, ssm_v, cw_v, cb_v, xp_v, gain_v, dtp_v, dtb_v, alog_v, dskip_v,
    q_v, nkv_v, pool_v, sel_s, len_s,
    q_own, q_all, sel_all, y_send, y_recv, z_send, zb_send, z_recv, zb_recv, g_recv,
    p_send, pl_send, p_recv, pl_recv, yout,
    load_sem, q_ss, q_rs, c_ss, c_rs, f_ss, fc_ss, y_ss, y_rs, z_ss, z_rs, zb_ss, zb_rs, g_ss, g_rs, p_ss, p_rs, pl_ss, pl_rs,
):
    r = lax.axis_index("req")
    h = lax.axis_index("head")
    c = lax.axis_index("ctx")

    def zpeer(i):
        return (r, h, lax.rem(c + i, NZ))

    def ypeer(i):
        return (r, lax.rem(h + i, NY), c)

    def send(src, dst, ss, rs, dev):
        pltpu.make_async_remote_copy(
            src_ref=src, dst_ref=dst, send_sem=ss, recv_sem=rs, device_id=dev, device_id_type=MESH
        ).start()

    def drain(ref, sem):
        pltpu.make_async_copy(ref, ref, sem).wait()

    is_early = c < EARLY
    is_late = c >= EARLY
    mine = c - APART
    is_hub = (mine >= 0) & (mine < EARLY)
    is_rest = is_late & jnp.logical_not(is_hub)

    def target_of(i):
        return lax.rem(c + i, NZ)

    barrier = pltpu.get_barrier_semaphore()

    def greet(dev):
        pl.semaphore_signal(barrier, inc=1, device_id=dev, device_id_type=MESH)

    for i in FAR_FIRST:
        pl.when(is_early | (target_of(i) >= EARLY) | (is_hub & (target_of(i) == mine)))(functools.partial(greet, zpeer(i)))
    for i in range(1, NY):
        greet(ypeer(i))

    pairs = (
        (q_h, q_v), (sel_h, sel_s), (len_h, len_s), (xz_h, xz_v), (cs_h, cs_v), (cw_h, cw_v), (cb_h, cb_v),
        (xp_h, xp_v), (nkv_h, nkv_v), (pool_h, pool_v), (dtp_h, dtp_v), (gain_h, gain_v),
        (dtb_h, dtb_v), (alog_h, alog_v), (dskip_h, dskip_v), (ssm_h, ssm_v),
    )
    loads = [pltpu.make_async_copy(a, b, load_sem.at[k]) for k, (a, b) in enumerate(pairs)]
    for cp in loads:
        cp.start()

    loads[0].wait()
    qrow = q_v[0:1, :].astype(F32)
    for k in range(16):
        q_own[k : k + 1, :] = qrow[:, k * HEAD_DIM : (k + 1) * HEAD_DIM]
    q_all[c] = q_own[...].astype(BF16)

    loads[1].wait()
    loads[2].wait()
    lane = lax.broadcasted_iota(jnp.int32, (1, 128), 1)
    listed = jnp.where(lane == TOPK, len_s[0, 0], -1)
    for k in range(TOPK):
        listed = jnp.where(lane == k, sel_s[0, k], listed)
    sel_all[c] = listed
    z_recv[c] = jnp.zeros((16, 128), BF16)
    zb_recv[c] = jnp.zeros((1, 128), F32)

    for e in range(EARLY):

        @pl.when(is_late & (mine != e))
        def _():
            z_recv[e] = jnp.zeros((16, 128), BF16)
            zb_recv[e] = jnp.zeros((1, 128), F32)

    for k in (3, 4, 5, 6):
        loads[k].wait()
    conv = cb_v[0:1, :] + cw_v[3:4, :] * xz_v[:, 0, :].astype(F32)
    for k in range(3):
        conv = conv + cw_v[k : k + 1, :] * cs_v[k].astype(F32)
    mixed_bf = silu(conv).astype(BF16)
    loads[7].wait()
    for j in range(4):
        part = lax.dot_general(mixed_bf, xp_v[j * 128 : (j + 1) * 128, :], NT, preferred_element_type=F32)
        for k in range(NY):
            y_send[k, 4 * j : 4 * j + 4, :] = part[4 * k : 4 * k + 4, :]
    part = lax.dot_general(mixed_bf, xp_v[DT_RANK : DT_RANK + 32, :], NT, preferred_element_type=F32)
    for k in range(NY):
        y_send[k, 16:17, :] = jnp.concatenate([part[4 * k + i : 4 * k + i + 1, :] for i in range(4)], axis=1)

    loads[8].wait()
    nkv = nkv_v[0:1, :].astype(F32)
    half = lax.broadcasted_iota(jnp.int32, (16, HEAD_DIM), 0) < 8
    own_key = jnp.where(half, nkv[:, 0:128], nkv[:, 256:384])
    own_value = jnp.where(half, nkv[:, 128:256], nkv[:, 384:512])
    own_score = jnp.sum(q_own[...] * own_key, axis=1, keepdims=True) * SCALE2
    tokens = POOL * PAGE
    low_half = lane < PAGE
    token = jnp.where(low_half, lane, lane - PAGE)
    entry = jnp.where(lane < POOL, c * POOL + lane, -1)
    for k in range(9, 16):
        loads[k].wait()
    gain = jnp.concatenate(
        [jnp.broadcast_to(gain_v[0:1, j * 128 : (j + 1) * 128], (4, 128)) for j in range(4)], axis=0
    )

    pl.semaphore_wait(barrier, jnp.where(is_early, EARLY, NZ - 1) + NY - 1)

    for i in range(1, NY):
        send(y_send.at[lax.rem(h + i, NY)], y_recv.at[i - 1], y_ss, y_rs, ypeer(i))

    def drain_rows(n, *pairs):
        for ref, sem in pairs:
            drain(ref.at[pl.ds(0, n)], sem)

    def send_query(dev, group):
        send(sel_all.at[c], sel_all.at[c], c_ss, c_rs.at[group], dev)
        send(q_all.at[c], q_all.at[c], q_ss, q_rs.at[group], dev)

    def each_early(act):
        for to in range(EARLY):
            pl.when(c != to)(functools.partial(act, (r, h, jnp.int32(to))))

    def each_late(act):
        for to in FORWARD_ORDER:
            if to >= EARLY:
                pl.when(c != to)(functools.partial(act, (r, h, jnp.int32(to))))

    @pl.when(is_early)
    def _():
        send_query((r, h, c + APART), 4)
        each_early(lambda dev: send_query(dev, 0))

    @pl.when(is_hub)
    def _():
        drain_rows(1, (q_all, q_rs.at[4]), (sel_all, c_rs.at[4]))

        def forward(dev):
            send(q_all.at[mine], q_all.at[mine], f_ss, q_rs.at[0], dev)
            send(sel_all.at[mine], sel_all.at[mine], fc_ss, c_rs.at[0], dev)

        each_late(forward)

    @pl.when(is_late)
    def _():
        for i in FAR_FIRST:
            send_query(zpeer(i), jnp.where(c < 4, 1, 2 + c // HALF))

    total = y_send[h]
    drain(y_recv, y_rs)
    for i in range(NY - 1):
        total = total + y_recv[i]
    z_send[0] = total[0:16].astype(BF16)
    zb_send[0] = total[16:17]

    def send_sums(dev, which, group):
        send(z_send.at[which], z_recv.at[c], z_ss, z_rs.at[group], dev)
        send(zb_send.at[which], zb_recv.at[c], zb_ss, zb_rs.at[group], dev)

    @pl.when(is_early)
    def _():
        send_sums((r, h, c + APART), 0, 2)
        each_early(lambda dev: send_sums(dev, 0, 0))

    @pl.when(is_hub)
    def _():
        drain_rows(1, (z_recv, z_rs.at[2]), (zb_recv, zb_rs.at[2]))
        z_send[1] = (total[0:16] + z_recv[mine].astype(F32)).astype(BF16)
        zb_send[1] = total[16:17] + zb_recv[mine]
        each_early(lambda dev: send_sums(dev, 0, 1))
        each_late(lambda dev: send_sums(dev, 1, 1))

    @pl.when(is_rest)
    def _():
        for to in range(EARLY):
            send_sums((r, h, jnp.int32(to)), 0, 1)
        for to in range(EARLY, NZ):
            pl.when(c != to)(functools.partial(send_sums, (r, h, jnp.int32(to)), 0, 1))

    own_total = total

    def finish_sums():
        total = own_total[0:16]
        terms = zb_send[0]
        if EARLY > 1:
            pl.when(is_early)(functools.partial(drain_rows, EARLY - 1, (z_recv, z_rs.at[0]), (zb_recv, zb_rs.at[0])))
        others = (z_recv, z_rs.at[1]), (zb_recv, zb_rs.at[1])
        pl.when(is_early)(functools.partial(drain_rows, NZ - EARLY, *others))
        pl.when(is_late)(functools.partial(drain_rows, NZ - EARLY - 1, *others))
        total = total + jnp.sum(z_recv[...].astype(F32), axis=0)
        terms = terms + jnp.sum(zb_recv[...], axis=0)
        square = total * total
        square = square[0:8] + square[8:16]
        square = square + jnp.concatenate([square[4:8], square[0:4]], axis=0)
        square = jnp.sum(square, axis=1, keepdims=True) * (1.0 / DT_RANK)
        inv = lax.rsqrt(square + EPS)
        g_recv[h, 0:16, :] = total * jnp.concatenate([inv, inv], axis=0) * gain
        g_recv[h, 16:17, :] = terms
        for i in range(1, NY):
            send(g_recv.at[h], g_recv.at[h], g_ss, g_rs, ypeer(i))

    diagonal = (
        lax.broadcasted_iota(jnp.int32, (1, 16, HEAD_DIM), 1)
        == lax.broadcasted_iota(jnp.int32, (1, 16, HEAD_DIM), 2)
    )
    for g, (first, last) in enumerate(GROUPS):
        n = last - first
        arrivals = (q_all, q_rs.at[g]), (sel_all, c_rs.at[g])
        if g == 0:
            pl.when(is_rest)(functools.partial(drain_rows, EARLY, *arrivals))
            if EARLY > 1:
                pl.when(is_early | is_hub)(functools.partial(drain_rows, EARLY - 1, *arrivals))
        else:
            if g == 3:
                pl.when(is_early)(finish_sums)
            inside = (c >= first) & (c < last)
            pl.when(inside)(functools.partial(drain_rows, n - 1, *arrivals))
            pl.when(jnp.logical_not(inside))(functools.partial(drain_rows, n, *arrivals))
        listed = sel_all[first:last, 0, :]
        counts = jnp.zeros((n, 128), jnp.int32)
        for k in range(TOPK):
            amount = listed[:, TOPK : TOPK + 1] if k == 0 else PAGE
            counts = jnp.where(listed[:, k : k + 1] == entry, amount, counts)
        bias = jnp.concatenate(
            [
                jnp.where(
                    token < jnp.where(low_half, counts[:, 2 * j : 2 * j + 1], counts[:, 2 * j + 1 : 2 * j + 2]),
                    0.0,
                    FAR_BELOW,
                )
                for j in range(POOL // 2)
            ],
            axis=1,
        )
        queries = q_all[first:last].astype(F32)
        outs, levels = [], []
        for v in range(2):
            qv = queries[:, 8 * v : 8 * v + 8, :].reshape(n * 8, HEAD_DIM).astype(BF16)
            keys = pool_v[:, :, 256 * v : 256 * v + 128].reshape(tokens, HEAD_DIM)
            values = pool_v[:, :, 256 * v + 128 : 256 * v + 256].reshape(tokens, HEAD_DIM)
            s = lax.dot_general(qv, keys, NT, preferred_element_type=F32) * SCALE2
            s = s.reshape(n, 8, tokens) + bias[:, None, :]
            top = jnp.maximum(jnp.max(s, axis=2, keepdims=True), FLOOR)
            w = jnp.exp2(s - top).astype(BF16)
            weight_sum = jnp.sum(w.astype(F32), axis=2, keepdims=True)
            o = jnp.dot(w.reshape(n * 8, tokens), values, preferred_element_type=F32).reshape(n, 8, HEAD_DIM)
            kept = jnp.maximum(weight_sum, 1.0)
            outs.append(o / kept)
            levels.append(top + jnp.log2(kept))
        level = jnp.concatenate(levels, axis=1)
        p_send[first:last] = jnp.concatenate(outs, axis=1).astype(BF16)
        pl_send[first:last] = jnp.sum(jnp.where(diagonal, level, 0.0), axis=1, keepdims=True)

        def send_part(to):
            dev = (r, h, jnp.int32(to))
            send(p_send.at[to], p_recv.at[c], p_ss, p_rs.at[c // HALF], dev)
            send(pl_send.at[to], pl_recv.at[c], pl_ss, pl_rs.at[c // HALF], dev)

        for to in range(first, last):
            pl.when(c != to)(functools.partial(send_part, to))

    pl.when(is_late)(finish_sums)
    rate = jnp.exp(alog_v[...])
    gate = silu(xz_v[:, 1, :].astype(F32))
    mixed = mixed_bf.astype(F32)
    drain(y_recv, g_rs)

    step = dtb_v[0:1, :]
    for j in range(4):
        normed = jnp.concatenate([g_recv[k, 4 * j : 4 * j + 4, :] for k in range(NY)], axis=0).astype(BF16)
        step = step + jnp.dot(normed, dtp_v[j * 128 : (j + 1) * 128, :], preferred_element_type=F32)
    step = jnp.maximum(step, 0.0) + jnp.log1p(jnp.exp(-jnp.abs(step)))
    terms = jnp.concatenate([g_recv[k, 16:17, :] for k in range(NY)] + [jnp.zeros((124, 128), F32)], axis=0).T
    drive = step * mixed
    for i in range(16):
        k, low = i // 4, 32 * (i % 4)
        decay = jnp.exp(-(step[i : i + 1, :] * rate))
        new = decay * ssm_v[i] + drive[i : i + 1, :] * terms[low : low + 16, k : k + 1]
        state_v[i] = new
        yout[i : i + 1, :] = jnp.sum(terms[low + 16 : low + 32, k : k + 1] * new, axis=0, keepdims=True)
    mamba_v[...] = ((yout[...] + dskip_v[0:1, :] * mixed) * gate).astype(BF16)

    p_recv[c] = p_send[c]
    pl_recv[c] = pl_send[c]
    top, weight, summed = own_score, jnp.ones_like(own_score), own_value
    for g, (first, last) in enumerate(((0, HALF), (HALF, NZ))):
        arrivals = (pl_recv, pl_rs.at[g]), (p_recv, p_rs.at[g])
        pl.when(c // HALF == g)(functools.partial(drain_rows, HALF - 1, *arrivals))
        pl.when(c // HALF != g)(functools.partial(drain_rows, HALF, *arrivals))
        level = jnp.sum(jnp.where(diagonal, pl_recv[first:last], 0.0), axis=2, keepdims=True)
        new_top = jnp.maximum(top, jnp.max(level, axis=0))
        old = jnp.exp2(top - new_top)
        w = jnp.exp2(level - new_top[None])
        weight = weight * old + jnp.sum(w, axis=0)
        summed = summed * old + jnp.sum(w * p_recv[first:last].astype(F32), axis=0)
        top = new_top
    joined = (summed / weight).astype(BF16)
    for k in range(16):
        attn_v[0:1, k * HEAD_DIM : (k + 1) * HEAD_DIM] = joined[k : k + 1, :]

    drain(y_recv, y_ss)
    drain(y_recv, g_ss)
    drain_rows(NZ - 1, (p_recv, p_ss), (pl_recv, pl_ss))
    sent = (q_all, q_ss), (sel_all, c_ss), (z_recv, z_ss), (zb_recv, zb_ss)
    pl.when(is_early)(functools.partial(drain_rows, EARLY, *sent))
    pl.when(is_late)(functools.partial(drain_rows, NZ - 1, *sent))

    pl.when(is_hub)(functools.partial(drain_rows, NZ - EARLY - 1, (q_all, f_ss), (sel_all, fc_ss)))


def hand_over(a_in, b_in, c_in, a_out, b_out, c_out, sem):
    copies = [
        pltpu.make_async_copy(x, y, sem.at[k])
        for k, (x, y) in enumerate(((a_in, a_out), (b_in, b_out), (c_in, c_out)))
    ]
    for cp in copies:
        cp.start()
    for cp in copies:
        cp.wait()


def on_device(
    xz, conv_state, ssm_state, conv_weight, conv_bias, x_proj, dt_norm_gain, dt_proj, dt_bias, a_log, d_skip,
    query, new_kv, kv_pool, page_sel, lengths,
):
    args = (
        xz, conv_state.transpose(1, 0, 2), ssm_state, conv_weight, conv_bias.reshape(1, -1), x_proj.T,
        dt_norm_gain.reshape(1, -1), dt_proj, dt_bias.reshape(1, -1), a_log, d_skip.reshape(1, -1),
        query, new_kv, kv_pool, page_sel, lengths.reshape(1, 1),
    )
    hbm = pl.BlockSpec(memory_space=pltpu.HBM)
    vmem = pl.BlockSpec(memory_space=pltpu.VMEM)
    outs = (((16, 256), BF16), ((16, STATE, 256), F32), ((1, 16 * HEAD_DIM), BF16))
    in_smem = {14, 15}
    scratch = [
        (pltpu.SMEM if k in in_smem else pltpu.VMEM)(a.shape, a.dtype) for k, a in enumerate(args)
    ]
    scratch += [
        pltpu.VMEM((16, HEAD_DIM), F32),
        pltpu.VMEM((NZ, 16, HEAD_DIM), BF16),
        pltpu.VMEM((NZ, 1, 128), jnp.int32),
        pltpu.VMEM((NY, 17, 128), F32),
        pltpu.VMEM((NY - 1, 17, 128), F32),
        pltpu.VMEM((2, 16, 128), BF16),
        pltpu.VMEM((2, 1, 128), F32),
        pltpu.VMEM((NZ, 16, 128), BF16),
        pltpu.VMEM((NZ, 1, 128), F32),
        pltpu.VMEM((NY, 17, 128), F32),
        pltpu.VMEM((NZ, 16, HEAD_DIM), BF16),
        pltpu.VMEM((NZ, 1, 128), F32),
        pltpu.VMEM((NZ, 16, HEAD_DIM), BF16),
        pltpu.VMEM((NZ, 1, 128), F32),
        pltpu.VMEM((16, 256), F32),
        pltpu.SemaphoreType.DMA((len(args),)),
    ]
    one, two = pltpu.SemaphoreType.DMA, pltpu.SemaphoreType.DMA((2,))
    three = pltpu.SemaphoreType.DMA((3,))
    four = pltpu.SemaphoreType.DMA((5,))
    scratch += [one, four, one, four, one, one, one, one, one, three, one, three, one, one, one, two, one, two]
    made = pl.pallas_call(
        kernel,
        out_shape=[pltpu.VMEM(*o) for o in outs],
        in_specs=[hbm] * len(args),
        out_specs=[vmem] * 3,
        scratch_shapes=scratch,
        name="decode_step",
        compiler_params=pltpu.CompilerParams(
            collective_id=0, has_side_effects=True, vmem_limit_bytes=60 * 2**20
        ),
    )(*args)
    return pl.pallas_call(
        hand_over,
        out_shape=[jax.ShapeDtypeStruct(*o) for o in outs],
        in_specs=[vmem] * 3,
        out_specs=[hbm] * 3,
        scratch_shapes=[pltpu.SemaphoreType.DMA((3,))],
        name="hand_over",
        compiler_params=pltpu.CompilerParams(vmem_limit_bytes=4 * 2**20),
    )(*made)


def solution(mesh):
    placed = (
        P("req", None, ("head", "ctx")),
        P("req", None, ("head", "ctx")),
        P("req", None, ("head", "ctx")),
        P(None, ("head", "ctx")),
        P(("head", "ctx")),
        P(("head", "ctx"), None),
        P(),
        P(None, ("head", "ctx")),
        P(("head", "ctx")),
        P(None, ("head", "ctx")),
        P(("head", "ctx")),
        P(("req", "ctx"), "head"),
        P(("req", "ctx"), "head"),
        P(("req", "ctx"), None, "head"),
        P(("req", "ctx"), None),
        P(("req", "ctx")),
    )
    return jax.shard_map(
        on_device,
        mesh=mesh,
        in_specs=placed,
        out_specs=(
            P("req", ("head", "ctx")),
            P("req", None, ("head", "ctx")),
            P(("req", "ctx"), "head"),
        ),
        check_vma=False,
    )
```
